32 devices in a mesh: dp: 4 (over y, x), expert: 8 (over z, core).
Axes of the slice: x: 2, y: 2, z: 4, core: 2. Of those that a mesh axis runs over, the one named last changes fastest.
Arguments:
- cotangent: bfloat16 [4096, 4096], P(('dp', 'expert')), may hold values from -0.59765625 to 0.59765625
- expert_ids: int32 [4096, 8], P(('dp', 'expert')), may hold values from 0 to 15, all different within a row; in each aligned block of 128 rows (0 to 127, 128 to 255, ...) at most 80 rows name the same one
- gates: bfloat16 [4096, 8], P(('dp', 'expert')), may hold values from 0.019897461 to 0.5
- hidden: bfloat16 [16, 4, 640, 1536], P('expert', 'dp'), may hold values from -6 to 6
- q_prev: bfloat16 [16, 4096, 64], P('expert', 'dp'), may hold values from -0.09375 to 0.09375
Outputs:
- p_merged: float32 [16, 1536, 64], P('expert', 'dp')
- q_next: float32 [16, 4096, 64], P('expert', 'dp')
The draws below stay inside these ranges and needn't reach their ends.
Inputs may be any that keep to these rules, and one draw needn't show every extreme that they name: `expert_ids`: each row names 8 different experts. Within the 128 rows of one device no expert is named by more than 80 rows, a bound that some block reaches.
All inputs are finite; a program needn't handle non-finite values.
Results may differ from the reference program's by a relative error of at most 0.0056.
Values may be sent and summed in bfloat16 or wider, within the bound.
No kernel may reach another device: no remote copies, remote signals or barrier semaphores. Data moves between devices by JAX's collectives and lax.ppermute only.
A program may use at most 128 MiB of HBM per device.

```python
import math
import jax
import jax.numpy as jnp
import numpy as np
from jax import lax

D = 4096
FF = 1536
TOP = 8
RANK = 64
TOK_DEV = 128
EXPERTS = 16
CAP = 80
SLOTS = 640
TOKENS = 4096
N_DP = 4
N_EXPERT = 8


def block_scale(own_key, shape, split, least, high):
    gain, own = 1.0, jax.random.fold_in(own_key, 6)
    for dim, shards_of in split:
        heights = jnp.exp(jax.random.uniform(jax.random.fold_in(own, dim), (shards_of,), jnp.float32, least / len(split), high / len(split)))
        gain = gain * jnp.repeat(heights, shape[dim] // shards_of).reshape([-1 if axis == dim else 1 for axis in range(len(shape))])
    return gain


def assign_block(stream_key, own, number, rows, count, top, reach, lean):
    sequence = jax.random.permutation(stream_key, count)
    heavy_load, usual = portions_of(count, rows * top, reach, lean, True), portions_of(count, rows * top, reach, lean, False)
    places = jnp.arange(count)

    def named(sizes, offset_by):
        used = int((sizes > 0).sum())
        fixed = max(1, used // 4)
        moved = fixed + (places - fixed + offset_by * (used - fixed)) % max(1, count - fixed)
        return jnp.zeros((count,), jnp.int32).at[sequence[jnp.where(places < fixed, places, moved)]].set(jnp.asarray(sizes, jnp.int32))

    sizes = jnp.where(number % 4 == 0, named(heavy_load, number // 4), named(usual, number - number // 4 - 1))
    mixed = jax.random.permutation(jax.random.fold_in(own, 3), count)
    donor, sink = mixed[0:count // 2 * 2:2], mixed[1:count // 2 * 2:2]
    room = jnp.minimum(sizes[donor] - 1, reach - sizes[sink]) // 2
    room = jnp.where((donor == sequence[0]) | (sink == sequence[0]) | (sizes[sink] == 0), 0, jnp.maximum(room, 0))
    moved = jax.random.randint(jax.random.fold_in(own, 4), (count // 2,), 0, 1 << 20) % (room + 1)
    sizes = sizes.at[donor].add(-moved).at[sink].add(moved)
    members = jnp.searchsorted(jnp.cumsum(sizes), jnp.arange(rows * top), side="right").astype(jnp.int32)
    grid = members.reshape(top, rows).T
    grid = grid[jax.random.permutation(jax.random.fold_in(own, 1), rows)]
    offset_by = jax.random.randint(jax.random.fold_in(own, 2), (rows, 1), 0, top)
    return jnp.take_along_axis(grid, (jnp.arange(top)[None, :] + offset_by) % top, axis=1)


def portions_of(number_of, total, reach, skew, full):
    portions = [(1 << 20) // math.isqrt(grade ** skew) + 1 for grade in range(1, number_of + 1)]
    largest = reach if full else min(reach, max(-(-total // number_of), total * portions[0] // sum(portions)))
    least = 1 if total - largest >= number_of - 1 else 0
    counts, spare = [largest] + [least] * (number_of - 1), total - largest - least * (number_of - 1)
    while spare > 0:
        candidates = [i for i in range(1, number_of) if counts[i] < largest] or [i for i in range(1, number_of) if counts[i] < reach]
        whole, remaining = sum([portions[i] for i in candidates]), spare
        for i in candidates:
            extra = min(reach - counts[i], max(1, remaining * portions[i] // whole), spare)
            counts[i] = counts[i] + extra
            spare = spare - extra
    return np.array(counts)


def normal_values(stream_key, dims, scale, limit, pieces=(), kind=jnp.bfloat16):
    result = scale * jax.random.normal(stream_key, dims, jnp.float32)
    if pieces:
        result = result * block_scale(stream_key, dims, pieces, -0.22, 0.18)
    return jnp.clip(result, -limit, limit).astype(kind)


def setup_inputs(seed: int = 0) -> dict:
    key_of = jax.random.split(jax.random.key(seed), 6)
    cotangent = normal_values(key_of[0], (TOKENS, D), 0.1, 0.59765625, ((0, 32),))
    expert_ids_keys = jax.random.split(jax.random.fold_in(key_of[1], 1), TOKENS // TOK_DEV)
    expert_ids_turns = jax.random.permutation(jax.random.fold_in(key_of[1], 3), TOKENS // TOK_DEV)
    expert_ids = jax.vmap(lambda own, number: assign_block(jax.random.fold_in(key_of[1], 2), own, number, TOK_DEV, EXPERTS, TOP, CAP, 2))(expert_ids_keys, expert_ids_turns).reshape((TOKENS, TOP))
    gates = jnp.clip(jnp.exp(math.log(0.5) - 3.224016 * jax.random.uniform(key_of[2], (TOKENS, TOP), jnp.float32) ** block_scale(key_of[2], (TOKENS, TOP), ((0, 32),), -0.2, 0.2)), 0.019897461, 0.5).astype(jnp.bfloat16)
    hidden = normal_values(key_of[3], (EXPERTS, N_DP, SLOTS, FF), 1.0, 6.0, ((0, 8), (1, 4)))
    q_prev = normal_values(key_of[4], (EXPERTS, D, RANK), D ** -0.5, 0.09375, ((0, 8), (1, 4)))
    return {"cotangent": cotangent, "expert_ids": expert_ids, "gates": gates, "hidden": hidden, "q_prev": q_prev}


def reference(cotangent, expert_ids, gates, hidden, q_prev):
    blocks = N_DP * N_EXPERT
    per_block = TOK_DEV * TOP
    block_ids = expert_ids.reshape(blocks, per_block)
    labels = jnp.arange(EXPERTS, dtype=jnp.int32)
    onehot = (block_ids[:, :, None] == labels[None, None, :]).astype(jnp.int32)
    earlier = jnp.cumsum(onehot, axis=1) - onehot
    slot_index = jnp.sum(earlier * onehot, axis=2).astype(jnp.int32)
    block_index = jnp.arange(blocks, dtype=jnp.int32)[:, None]
    token_index = block_index * TOK_DEV + jnp.arange(per_block, dtype=jnp.int32)[None, :] // TOP
    row_key = (block_ids * (blocks * CAP) + block_index * CAP + slot_index).reshape(-1)
    row_total = EXPERTS * blocks * CAP
    token_rows = jnp.zeros((row_total,), jnp.int32).at[row_key].set(token_index.reshape(-1).astype(jnp.int32))
    gate_rows = jnp.zeros((row_total,), jnp.float32).at[row_key].set(gates.reshape(-1).astype(jnp.float32))
    token_rows = token_rows.reshape(EXPERTS, blocks * CAP)
    gate_rows = gate_rows.reshape(EXPERTS, blocks * CAP)

    def one_expert(expert_items):
        token_part, gate_part, hidden_part, factor = expert_items
        dispatched = (gate_part[:, None] * cotangent[token_part].astype(jnp.float32)).astype(jnp.bfloat16)
        projected = jnp.dot(dispatched.astype(jnp.float32), factor.astype(jnp.float32), preferred_element_type=jnp.float32).astype(jnp.bfloat16)
        hidden_rows = hidden_part.reshape(blocks * CAP, FF)
        merged = jnp.dot(hidden_rows.T.astype(jnp.float32), projected.astype(jnp.float32), preferred_element_type=jnp.float32)
        gram_matrix = jnp.dot(merged.T, merged, precision=lax.Precision.HIGHEST)
        lower_factor = jnp.linalg.cholesky(gram_matrix)
        solved = jax.scipy.linalg.solve_triangular(lower_factor, merged.T, lower=True)
        basis_rows = solved.T.astype(jnp.bfloat16)
        mapped = jnp.dot(hidden_rows.astype(jnp.float32), basis_rows.astype(jnp.float32), preferred_element_type=jnp.float32).astype(jnp.bfloat16)
        q_summed = jnp.dot(dispatched.T.astype(jnp.float32), mapped.astype(jnp.float32), preferred_element_type=jnp.float32)
        return (merged, q_summed)
    p_merged, q_next = lax.map(one_expert, (token_rows, gate_rows, hidden, q_prev))
    return (p_merged, q_next)
```

```python
import jax
import jax.numpy as jnp
from jax import lax
from jax.sharding import PartitionSpec as P

CORES = 2


def exchange(value, axis, distance):
    size = lax.axis_size(axis)
    return lax.ppermute(value, axis, [(i, i ^ distance) for i in range(size)])


def dense_gates(expert_ids, gates, experts_all):
    labels = jnp.arange(experts_all, dtype=jnp.int32)[:, None]
    dense = jnp.zeros((experts_all, expert_ids.shape[0]), jnp.bfloat16)
    for column in range(expert_ids.shape[1]):
        hit = labels == expert_ids[:, column][None, :]
        dense = dense + jnp.where(hit, gates[:, column][None, :], jnp.zeros((), jnp.bfloat16))
    return dense


def slot_choice(dense, capacity):
    tokens = dense.shape[-1]
    named = (dense > 0).astype(jnp.bfloat16)
    position = jnp.arange(tokens, dtype=jnp.int32)
    before = (position[:, None] < position[None, :]).astype(jnp.bfloat16)
    slot = jnp.einsum("...t,tu->...u", named, before, preferred_element_type=jnp.float32)
    slot = jnp.where(dense > 0, slot, -1.0).astype(jnp.int32)
    return slot[..., None, :] == jnp.arange(capacity, dtype=jnp.int32)[:, None]


def sum_over_dp(value):
    half = value.shape[-1] // 2
    distances = []
    step = 1
    while step < lax.axis_size("dp"):
        distances.append(step)
        step *= 2
    parts = [value[..., :half], value[..., half:]]
    for index in range(len(distances)):
        sent = []
        for part, order in zip(parts, (distances, distances[::-1])):
            rounded = part.astype(jnp.bfloat16)
            got = exchange(rounded, "dp", order[index])
            sent.append(rounded.astype(jnp.float32) + got.astype(jnp.float32))
        parts = sent
    return jnp.concatenate(parts, axis=-1)


def local(cotangent, expert_ids, gates, hidden, q_prev):
    members = lax.axis_size("dp")
    places = lax.axis_size("expert")
    chips = places // CORES
    held, _, slots, width = hidden.shape
    rank = q_prev.shape[2]
    tokens, model_width = cotangent.shape
    experts_all = held * places
    capacity = slots // places
    part = model_width // members
    my_dp = lax.axis_index("dp")
    my_place = lax.axis_index("expert")
    my_chip, my_core = my_place // CORES, my_place % CORES
    own_hidden = hidden[:, 0]

    dense = dense_gates(expert_ids, gates, experts_all)
    dense_pair = jnp.stack([dense, exchange(dense, "expert", 1)])

    factor = jnp.swapaxes(q_prev, 1, 2).reshape(held * rank, part)
    factors = [factor] + [exchange(factor, "expert", CORES * k) for k in range(1, chips)]

    columns = []
    for k in range(members):
        piece = lax.dynamic_slice_in_dim(cotangent, (my_dp ^ k) * part, part, 1)
        columns.append(exchange(piece, "dp", k) if k else piece)
    columns = jnp.stack(columns)
    columns_pair = jnp.stack([columns, exchange(columns, "expert", 1)])

    dense_groups = jnp.stack([dense] + [exchange(dense, "dp", k) for k in range(1, members)])
    gathered_gates = lax.all_gather(dense_groups, "expert", axis=1)
    gathered = lax.all_gather(columns, "expert", axis=1)

    flat_pair = columns_pair.reshape(-1, part)
    arrived = []
    for k in range(chips):
        y = lax.dot_general(
            flat_pair, factors[k], (((1,), (1,)), ((), ())), preferred_element_type=jnp.float32
        )
        y = y.astype(jnp.bfloat16).reshape(CORES, members, tokens, held * rank)
        total = y[:, 0].astype(jnp.float32)
        for d in range(1, members):
            total = total + exchange(y[:, d], "dp", d).astype(jnp.float32)
        owner = (my_chip ^ k) * CORES + my_core
        mine = lax.dynamic_slice_in_dim(dense_pair, owner * held, held, 1)
        weighted = total.reshape(CORES, tokens, held, rank) * jnp.swapaxes(mine, 1, 2).astype(
            jnp.float32
        )[..., None]
        choice = slot_choice(mine, capacity).astype(jnp.bfloat16)
        packed = jnp.einsum(
            "phct,pthr->pchr",
            choice,
            weighted.astype(jnp.bfloat16),
            preferred_element_type=jnp.float32,
        ).astype(jnp.bfloat16)
        packed = packed.reshape(CORES, capacity, held * rank)
        arrived.append(exchange(packed, "expert", CORES * k) if k else packed)
    arrived = jnp.stack(arrived)
    arrived = jnp.take(arrived, jnp.arange(chips) ^ my_chip, axis=0)
    arrived = jnp.take(arrived, jnp.arange(CORES) ^ my_core, axis=1)
    projected = arrived.reshape(slots, held, rank)

    partial_value = jnp.einsum(
        "shr,hsf->hrf", projected, own_hidden, preferred_element_type=jnp.float32
    )
    merged = sum_over_dp(partial_value)
    gram = jnp.einsum("hrf,hsf->hrs", merged, merged, precision=lax.Precision.HIGHEST)
    lower = jnp.linalg.cholesky(gram)
    basis = jax.vmap(
        lambda one, rhs: jax.scipy.linalg.solve_triangular(one, rhs, lower=True)
    )(lower, merged).astype(jnp.bfloat16)
    mapped = jnp.einsum(
        "hsf,hrf->shr", own_hidden, basis, preferred_element_type=jnp.float32
    ).astype(jnp.bfloat16)
    mapped = mapped.reshape(slots, held * rank)
    mapped_groups = jnp.stack([mapped] + [exchange(mapped, "dp", k) for k in range(1, members)])

    own_gates = lax.dynamic_slice_in_dim(gathered_gates, my_place * held, held, 2)
    choice = jnp.where(
        slot_choice(own_gates, capacity), own_gates[..., None, :], jnp.zeros((), jnp.bfloat16)
    )
    dispatched = jnp.einsum(
        "gphct,gptd->hgpcd", choice, gathered, preferred_element_type=jnp.float32
    ).astype(jnp.bfloat16)
    q_next = jnp.einsum(
        "gshr,hgsd->hrd",
        mapped_groups.reshape(members, slots, held, rank),
        dispatched.reshape(held, members, slots, part),
        preferred_element_type=jnp.float32,
    )
    share = width // members
    p_share = lax.dynamic_slice_in_dim(merged, my_dp * share, share, 2)
    return (jnp.swapaxes(p_share, 1, 2), jnp.swapaxes(q_next, 1, 2))


def solution(mesh):
    placed = (
        P(("dp", "expert"), None),
        P(("dp", "expert"), None),
        P(("dp", "expert"), None),
        P("expert", "dp", None, None),
        P("expert", "dp", None),
    )
    return jax.shard_map(
        local,
        mesh=mesh,
        in_specs=placed,
        out_specs=(P("expert", "dp", None), P("expert", "dp", None)),
        check_vma=False,
    )
```

```python
import functools

import jax
import jax.numpy as jnp
from jax import lax
from jax.experimental import pallas as pl
from jax.experimental.pallas import tpu as pltpu
from jax.sharding import PartitionSpec as P

CORES = 2
VMEM = 24 << 20
HIGHEST = lax.Precision.HIGHEST
NT = (((1,), (1,)), ((), ()))
TN = (((0,), (0,)), ((), ()))


def exchange(value, axis, distance):
    size = lax.axis_size(axis)
    return lax.ppermute(value, axis, [(i, i ^ distance) for i in range(size)])


def shift(value, axis, distance):
    size = lax.axis_size(axis)
    return lax.ppermute(value, axis, [(i, (i + distance) % size) for i in range(size)])


def dense_gates(expert_ids, gates, experts_all):
    labels = jnp.arange(experts_all, dtype=jnp.int32)[:, None]
    dense = jnp.zeros((experts_all, expert_ids.shape[0]), jnp.bfloat16)
    for column in range(expert_ids.shape[1]):
        hit = labels == expert_ids[:, column][None, :]
        dense = dense + jnp.where(hit, gates[:, column][None, :], jnp.zeros((), jnp.bfloat16))
    return dense


def sum_steps(members):
    distances = []
    step = 1
    while step < members:
        distances.append(step)
        step *= 2
    return distances, distances[::-1]


def slots_of(gates):
    tokens = gates.shape[1]
    before = (
        lax.broadcasted_iota(jnp.int32, (tokens, tokens), 0)
        < lax.broadcasted_iota(jnp.int32, (tokens, tokens), 1)
    ).astype(jnp.bfloat16)
    named = (gates > 0).astype(jnp.bfloat16)
    slot = jnp.dot(named, before, preferred_element_type=jnp.float32)
    return jnp.where(gates > 0, slot, -1.0)


def block_of(ref, group, sizes):
    members, tokens, _, _, experts_all = sizes
    chunks = ref.shape[1] // tokens
    start = group * tokens
    gate_row = members * tokens + group // chunks * experts_all
    gate_lane = group % chunks * tokens
    if not isinstance(group, int):
        start = pl.multiple_of(start, tokens)
        gate_row = pl.multiple_of(gate_row, 16)
        gate_lane = pl.multiple_of(gate_lane, tokens)
    return (
        ref[pl.ds(start, tokens), :],
        ref[pl.ds(gate_row, experts_all), pl.ds(gate_lane, tokens)],
    )


def for_each(count, body):
    if count <= 4:
        for index in range(count):
            body(index)
        return

    def step(index, carry):
        body(index)
        return carry

    lax.fori_loop(0, count, step, 0)


def project_kernel(sizes, halves, place_ref, *refs):
    members, tokens, held, rank, experts_all = sizes
    blocks, factors = refs[: 2 * halves], refs[2 * halves : -2]
    out_ref, stacked_ref = refs[-2:]
    chips, padded = len(factors), out_ref.shape[3]
    wide = held * rank
    for k in range(chips):
        stacked_ref[k * wide : (k + 1) * wide] = factors[k][...]
    index = lax.broadcasted_iota(jnp.int32, (chips * held, experts_all), 0)
    owner = ((place_ref[0] ^ (index // held)) * CORES + place_ref[1]) * held + index % held
    pick = (lax.broadcasted_iota(jnp.int32, owner.shape, 1) == owner).astype(jnp.bfloat16)
    row = lax.broadcasted_iota(jnp.int32, (padded, tokens), 0).astype(jnp.float32)
    lane = lax.broadcasted_iota(jnp.int32, (padded, wide), 1)

    def one_block(ref, group, out_group, core):
        columns, dense = block_of(ref, group, sizes)
        gates = jnp.dot(pick, dense, preferred_element_type=jnp.float32)
        slot = slots_of(gates)
        y = lax.dot_general(stacked_ref[...], columns, NT, preferred_element_type=jnp.float32)
        for k in range(chips):
            weighted, choice = [], []
            for i in range(k * held, (k + 1) * held):
                weighted.append(y[i * rank : (i + 1) * rank] * gates[i : i + 1])
                choice.append(jnp.where(slot[i : i + 1] == row, 1.0, 0.0))
            full = lax.dot_general(
                jnp.concatenate(choice).astype(jnp.bfloat16),
                jnp.concatenate(weighted).astype(jnp.bfloat16),
                NT,
                preferred_element_type=jnp.float32,
            )
            packed = full[:padded]
            for h in range(1, held):
                packed = jnp.where(lane >= h * rank, full[h * padded : (h + 1) * padded], packed)
            out_ref[out_group, k, core] = packed.astype(jnp.bfloat16)

    for half in range(halves):
        for core in range(CORES):
            ref = blocks[half * CORES + core]
            for_each(
                members,
                functools.partial(
                    lambda ref, half, core, g: one_block(ref, g, half * members + g, core),
                    ref,
                    half,
                    core,
                ),
            )


def project(place, blocks, factors, sizes, padded):
    members, tokens, held, rank, _ = sizes
    wide = held * rank
    chips, halves = len(factors), len(blocks) // CORES
    return pl.pallas_call(
        functools.partial(project_kernel, sizes, halves),
        out_shape=jax.ShapeDtypeStruct(
            (halves * members, chips, CORES, padded, wide), jnp.bfloat16
        ),
        in_specs=[pl.BlockSpec(memory_space=pltpu.SMEM)]
        + [pl.BlockSpec(memory_space=pltpu.VMEM)] * (len(blocks) + chips),
        out_specs=pl.BlockSpec(memory_space=pltpu.VMEM),
        scratch_shapes=[pltpu.VMEM((chips * wide, blocks[0].shape[1]), jnp.bfloat16)],
        compiler_params=pltpu.CompilerParams(vmem_limit_bytes=VMEM),
    )(place, *blocks, *factors)


def left_kernel(place_ref, *refs):
    arrived, hidden_ref, outs, rows_ref = refs[:-4], refs[-4], refs[-3:-1], refs[-1]
    for k, ref in enumerate(arrived):
        base = (place_ref[0] ^ k) * CORES
        rows_ref[base + place_ref[1]] = ref[0]
        rows_ref[base + 1 - place_ref[1]] = ref[1]
    places, capacity, wide = rows_ref.shape
    held = hidden_ref.shape[0]
    rank = wide // held
    rows = rows_ref[...].reshape(places * capacity, wide)
    half = outs[0].shape[1]
    for h in range(held):
        for index, out_ref in enumerate(outs):
            product = lax.dot_general(
                rows,
                hidden_ref[h, :, index * half : (index + 1) * half],
                TN,
                preferred_element_type=jnp.float32,
            )
            out_ref[h * rank : (h + 1) * rank] = product[h * rank : (h + 1) * rank].astype(
                jnp.bfloat16
            )


def left_partial(place, arrived, own_hidden, capacity):
    held, slots, width = own_hidden.shape
    _, padded, wide = arrived[0].shape
    if padded != capacity:
        chips = len(arrived)
        rows = jnp.take(jnp.stack(arrived), jnp.arange(chips) ^ place[0], axis=0)
        rows = jnp.take(rows, jnp.arange(CORES) ^ place[1], axis=1)[:, :, :capacity]
        rows = rows.reshape(slots, held, wide // held)
        value = jnp.einsum("shr,hsf->hrf", rows, own_hidden, preferred_element_type=jnp.float32)
        value = value.reshape(wide, width).astype(jnp.bfloat16)
        return [value[:, : width // 2], value[:, width // 2 :]]
    shape = jax.ShapeDtypeStruct((wide, width // 2), jnp.bfloat16)
    return pl.pallas_call(
        left_kernel,
        out_shape=(shape, shape),
        in_specs=[pl.BlockSpec(memory_space=pltpu.SMEM)]
        + [pl.BlockSpec(memory_space=pltpu.VMEM)] * (len(arrived) + 1),
        out_specs=(pl.BlockSpec(memory_space=pltpu.VMEM),) * 2,
        scratch_shapes=[pltpu.VMEM((slots // capacity, capacity, wide), jnp.bfloat16)],
        compiler_params=pltpu.CompilerParams(vmem_limit_bytes=VMEM),
    )(place, *arrived, own_hidden)


def whiten_kernel(first_ref, first_got_ref, last_ref, last_got_ref, hidden_ref, mapped_ref, merged_ref):
    held, rank, width = merged_ref.shape
    half = width // 2
    for h in range(held):
        rows = slice(h * rank, (h + 1) * rank)
        merged_ref[h, :, :half] = first_ref[rows].astype(jnp.float32) + first_got_ref[rows].astype(
            jnp.float32
        )
        merged_ref[h, :, half:] = last_ref[rows].astype(jnp.float32) + last_got_ref[rows].astype(
            jnp.float32
        )
    lane = lax.broadcasted_iota(jnp.int32, (8, 2 * rank), 1)
    row = lax.broadcasted_iota(jnp.int32, (8, 2 * rank), 0)
    blocks = rank // 8
    states = []
    for h in range(held):
        factor = merged_ref[h]
        gram = lax.dot_general(
            factor, factor, NT, precision=HIGHEST, preferred_element_type=jnp.float32
        )
        padded = jnp.concatenate([gram, jnp.zeros_like(gram)], axis=1)
        states.append(
            [
                jnp.where(lane == rank + 8 * b + row, 1.0, padded[8 * b : 8 * b + 8])
                for b in range(blocks)
            ]
        )
    for k in range(rank):
        first, inner = k // 8, k % 8
        for state in states:
            pivot_column = jnp.broadcast_to(state[first][:, k : k + 1], (8, 2 * rank))
            scaled = state[first][inner : inner + 1] / pivot_column[inner : inner + 1]
            for b in range(first, blocks):
                column = pivot_column
                if b == first:
                    column = jnp.where(row > inner, column, 0.0)
                else:
                    column = jnp.broadcast_to(state[b][:, k : k + 1], (8, 2 * rank))
                state[b] = state[b] - column * scaled
    for h in range(held):
        inverse = []
        for b, block in enumerate(states[h]):
            pivot = jnp.sum(jnp.where(lane == 8 * b + row, block, 0.0), axis=1, keepdims=True)
            inverse.append(block[:, rank:] / jnp.sqrt(pivot))
        inverse = jnp.concatenate(inverse, axis=0)
        basis = jnp.dot(
            inverse, merged_ref[h], precision=HIGHEST, preferred_element_type=jnp.float32
        ).astype(jnp.bfloat16)
        mapped_ref[:, h * rank : (h + 1) * rank] = lax.dot_general(
            hidden_ref[h], basis, NT, preferred_element_type=jnp.float32
        ).astype(jnp.bfloat16)


def whiten_and_map(parts, own_hidden):
    held, slots, width = own_hidden.shape
    wide = parts[0].shape[0]
    return pl.pallas_call(
        whiten_kernel,
        out_shape=(
            jax.ShapeDtypeStruct((slots, wide), jnp.bfloat16),
            jax.ShapeDtypeStruct((held, wide // held, width), jnp.float32),
        ),
        compiler_params=pltpu.CompilerParams(vmem_limit_bytes=VMEM),
    )(*parts, own_hidden)


def dispatch_kernel(sizes, place_ref, own_ref, other_ref, out_ref):
    members, tokens, held, _, experts_all = sizes
    padded = out_ref.shape[3]
    row = lax.broadcasted_iota(jnp.int32, (padded, tokens), 0).astype(jnp.float32)
    index = lax.broadcasted_iota(jnp.int32, (8, experts_all), 0)
    pick = lax.broadcasted_iota(jnp.int32, (8, experts_all), 1) == place_ref[0] * held + index
    pick = pick.astype(jnp.bfloat16)

    def one_group(g):
        for ref, core in ((own_ref, place_ref[1]), (other_ref, 1 - place_ref[1])):
            columns, dense = block_of(ref, g, sizes)
            gates = jnp.dot(pick, dense, preferred_element_type=jnp.float32)
            slot = slots_of(gates)
            choice = [
                jnp.where(slot[h : h + 1] == row, gates[h : h + 1], 0.0) for h in range(held)
            ]
            rows = jnp.dot(
                jnp.concatenate(choice).astype(jnp.bfloat16),
                columns,
                preferred_element_type=jnp.float32,
            ).astype(jnp.bfloat16)
            for h in range(held):
                out_ref[h, g, core] = rows[h * padded : (h + 1) * padded]

    for_each(members, one_group)


def dispatch(place, own, other, sizes, padded):
    members, tokens, held, _, _ = sizes
    return pl.pallas_call(
        functools.partial(dispatch_kernel, sizes),
        out_shape=jax.ShapeDtypeStruct(
            (held, members, CORES, padded, own.shape[1]), jnp.bfloat16
        ),
        in_specs=[pl.BlockSpec(memory_space=pltpu.SMEM)]
        + [pl.BlockSpec(memory_space=pltpu.VMEM)] * 2,
        out_specs=pl.BlockSpec(memory_space=pltpu.VMEM),
        compiler_params=pltpu.CompilerParams(vmem_limit_bytes=VMEM),
    )(place, own, other)


def right_kernel(steps, members, sources_ref, *refs):
    mapped, dispatched = refs[:members], refs[members : members + len(steps)]
    out_ref = refs[-1]
    held, groups, _, padded, part = dispatched[0].shape
    rank = out_ref.shape[1]
    if len(refs) > members + len(steps) + 1:
        out_ref[...] = refs[-2][...]
    else:
        out_ref[...] = jnp.zeros_like(out_ref)
    for (step, first), ref in zip(steps, dispatched):
        for g in range(groups):
            rows = mapped[first + g][pl.ds(sources_ref[step] * CORES, CORES)]
            rows = rows.reshape(CORES * padded, held * rank)
            for h in range(held):
                product = lax.dot_general(
                    rows,
                    ref[h, g].reshape(CORES * padded, part),
                    TN,
                    preferred_element_type=jnp.float32,
                )
                out_ref[h] += product[h * rank : (h + 1) * rank]


def right_factor(sources, mapped_groups, steps, dispatched, before=None):
    held, _, _, _, part = dispatched[0].shape
    rank = mapped_groups[0].shape[-1] // held
    operands = [*mapped_groups, *dispatched] + ([] if before is None else [before])
    return pl.pallas_call(
        functools.partial(right_kernel, steps, len(mapped_groups)),
        out_shape=jax.ShapeDtypeStruct((held, rank, part), jnp.float32),
        in_specs=[pl.BlockSpec(memory_space=pltpu.SMEM)]
        + [pl.BlockSpec(memory_space=pltpu.VMEM)] * len(operands),
        out_specs=pl.BlockSpec(memory_space=pltpu.VMEM),
        compiler_params=pltpu.CompilerParams(vmem_limit_bytes=VMEM),
    )(sources, *operands)


def local(cotangent, expert_ids, gates, hidden, q_prev):
    members = lax.axis_size("dp")
    places = lax.axis_size("expert")
    chips = places // CORES
    held, _, slots, width = hidden.shape
    rank = q_prev.shape[2]
    tokens, model_width = cotangent.shape
    experts_all = held * places
    capacity = slots // places
    padded = -(-capacity // 16) * 16
    part = model_width // members
    chunks = part // tokens
    halves = 2 if members > 1 else 1
    groups = members // halves
    sizes = (groups, tokens, held, rank, experts_all)
    my_dp = lax.axis_index("dp")
    my_place = lax.axis_index("expert")
    my_chip, my_core = my_place // CORES, my_place % CORES
    place = jnp.stack([my_chip, my_core]).astype(jnp.int32)
    own_place = jnp.stack([my_place, my_core]).astype(jnp.int32)
    own_hidden = hidden[:, 0]
    tie = lax.optimization_barrier

    def over_chips(blocks):
        return [shift(block, "expert", CORES) for block in blocks]

    def over_cores(blocks):
        return [exchange(block, "expert", 1) for block in blocks]

    def dispatch_half(blocks, others, half):
        return dispatch(own_place, blocks[half], others[half], sizes, padded)

    factor = jnp.swapaxes(q_prev, 1, 2).reshape(held * rank, part)
    factors = [factor] + [exchange(factor, "expert", CORES * k) for k in range(1, chips)]

    dense = dense_gates(expert_ids, gates, experts_all)
    tail = jnp.pad(dense, ((0, 0), (0, part - tokens)))
    pieces = []
    for k in range(members):
        piece = lax.dynamic_slice_in_dim(cotangent, (my_dp ^ k) * part, part, 1)
        piece = jnp.concatenate([piece, tail], axis=0)
        pieces.append(exchange(piece, "dp", k) if k else piece)
    pieces, factors = tie((pieces, factors))
    own = []
    for half in range(halves):
        mine = pieces[half * groups : (half + 1) * groups]
        tails = [piece[tokens:, :tokens] for piece in mine]
        while len(tails) % chunks:
            tails.append(jnp.zeros_like(tails[0]))
        tails = [jnp.concatenate(tails[i : i + chunks], 1) for i in range(0, len(tails), chunks)]
        own.append(jnp.concatenate([piece[:tokens] for piece in mine] + tails, axis=0))
    other = over_cores(own)
    ring = over_chips(own) if chips > 1 else None

    blocks = [block for pair in zip(own, other) for block in pair]
    y = project(place, blocks, factors, sizes, padded)
    got = [exchange(y[d], "dp", d) for d in range(1, members)]
    dispatched = [dispatch_half(own, other, half) for half in range(halves)]
    got, dispatched = tie((got, dispatched))
    summed = y[0].astype(jnp.float32)
    for value in got:
        summed = summed + value.astype(jnp.float32)
    summed = summed.astype(jnp.bfloat16)
    arrived = [summed[0]] + [exchange(summed[k], "expert", CORES * k) for k in range(1, chips)]
    steps = [(0, half * groups) for half in range(halves)]
    orders = sum_steps(members)
    rounds = len(orders[0])
    pending = []

    def advance(value, ring, step):
        value, ring = tie((value, ring))
        others = over_cores(ring)
        for half in range(halves):
            pending.append((step, half, ring, others))
        return value, (over_chips(ring) if step < chips - 1 else None)

    def fill(value):
        if not pending:
            return value
        step, half, blocks, others = pending.pop(0)
        done = dispatch_half(blocks, others, half)
        value, done = tie((value, done))
        dispatched.append(done)
        steps.append((step, half * groups))
        return value

    step = 1
    if chips > 1:
        arrived, ring = advance(arrived, ring, step)
        step += 1
    parts = left_partial(place, arrived, own_hidden, capacity)
    for index in range(rounds):
        got = [exchange(p, "dp", order[index]) for p, order in zip(parts, orders)]
        got = fill(got)
        if index < rounds - 1:
            parts = [
                (p.astype(jnp.float32) + q.astype(jnp.float32)).astype(jnp.bfloat16)
                for p, q in zip(parts, got)
            ]
    mapped, merged = whiten_and_map([parts[0], got[0], parts[1], got[1]], own_hidden)
    if ring is not None and step < chips:
        mapped, ring = advance(mapped, ring, step)
        step += 1
    mapped = mapped.reshape(places, capacity, held * rank)
    mapped = jnp.pad(mapped, ((0, 0), (0, padded - capacity), (0, 0)))
    gathered = [exchange(mapped, "dp", k) for k in range(1, members)]
    while pending:
        gathered = fill(gathered)
    mapped_groups = [mapped] + gathered
    sources = ((my_chip - jnp.arange(chips)) % chips).astype(jnp.int32)
    q_next = right_factor(sources, mapped_groups, steps, dispatched)
    while ring is not None and step < chips:
        q_next, ring = advance(q_next, ring, step)
        step += 1
        while pending:
            late, half, blocks, others = pending.pop(0)
            done = dispatch_half(blocks, others, half)
            q_next = right_factor(
                sources, mapped_groups, [(late, half * groups)], [done], q_next
            )
    share = width // members
    p_share = lax.dynamic_slice_in_dim(merged, my_dp * share, share, 2)
    return (jnp.swapaxes(p_share, 1, 2), jnp.swapaxes(q_next, 1, 2))


def solution(mesh):
    placed = (
        P(("dp", "expert"), None),
        P(("dp", "expert"), None),
        P(("dp", "expert"), None),
        P("expert", "dp", None, None),
        P("expert", "dp", None),
    )
    return jax.shard_map(
        local,
        mesh=mesh,
        in_specs=placed,
        out_specs=(P("expert", "dp", None), P("expert", "dp", None)),
        check_vma=False,
    )
```

```python
import functools

import jax
import jax.numpy as jnp
from jax import lax
from jax.experimental import pallas as pl
from jax.experimental.pallas import tpu as pltpu
from jax.sharding import PartitionSpec as P

CORES = 2
VMEM = 24 << 20
HIGHEST = lax.Precision.HIGHEST
NT = (((1,), (1,)), ((), ()))
TN = (((0,), (0,)), ((), ()))


def exchange(value, axis, distance):
    size = lax.axis_size(axis)
    return lax.ppermute(value, axis, [(i, i ^ distance) for i in range(size)])


def pieces_kernel(place_ref, cotangent_ref, ids_ref, gates_ref, *out_refs):
    tokens = cotangent_ref.shape[0]
    part = out_refs[0].shape[1]
    experts_all = out_refs[0].shape[0] - tokens
    label = lax.broadcasted_iota(jnp.int32, (experts_all, tokens), 0)
    dense = jnp.zeros((experts_all, tokens), jnp.float32)
    for k in range(ids_ref.shape[0]):
        gate = gates_ref[k : k + 1].astype(jnp.float32)
        dense = dense + jnp.where(label == ids_ref[k : k + 1], gate, 0.0)
    dense = dense.astype(jnp.bfloat16)
    for k, out_ref in enumerate(out_refs):
        start = pl.multiple_of((place_ref[0] ^ k) * part, part)
        out_ref[:tokens] = cotangent_ref[:, pl.ds(start, part)]
        out_ref[tokens:] = jnp.zeros((experts_all, part), jnp.bfloat16)
        out_ref[tokens:, :tokens] = dense


def cut_pieces(place, cotangent, expert_ids, gates, members, experts_all):
    tokens, model_width = cotangent.shape
    shape = jax.ShapeDtypeStruct(
        (tokens + experts_all, model_width // members), jnp.bfloat16
    )
    return pl.pallas_call(
        pieces_kernel,
        out_shape=(shape,) * members,
        in_specs=[pl.BlockSpec(memory_space=pltpu.SMEM)]
        + [pl.BlockSpec(memory_space=pltpu.VMEM)] * 3,
        out_specs=(pl.BlockSpec(memory_space=pltpu.VMEM),) * members,
        compiler_params=pltpu.CompilerParams(vmem_limit_bytes=VMEM),
    )(place, cotangent, jnp.swapaxes(expert_ids, 0, 1), jnp.swapaxes(gates, 0, 1))


def sum_steps(members):
    distances = []
    step = 1
    while step < members:
        distances.append(step)
        step *= 2
    return distances, distances[::-1]


def slots_of(gates):
    tokens = gates.shape[1]
    before = (
        lax.broadcasted_iota(jnp.int32, (tokens, tokens), 0)
        < lax.broadcasted_iota(jnp.int32, (tokens, tokens), 1)
    ).astype(jnp.bfloat16)
    named = (gates > 0).astype(jnp.bfloat16)
    slot = jnp.dot(named, before, preferred_element_type=jnp.float32)
    return jnp.where(gates > 0, slot, -1.0)


def aligned(value, multiple):
    return value if isinstance(value, int) else pl.multiple_of(value, multiple)


def columns_of(ref, first, group, sizes):
    tokens = sizes[1]
    return ref[pl.ds(aligned(first + group * tokens, 16), tokens), :]


def gates_of(ref, group, sizes):
    _, tokens, _, _, experts_all = sizes
    chunks = ref.shape[1] // tokens
    row = aligned(group // chunks * experts_all, 16)
    return ref[pl.ds(row, experts_all), pl.ds(aligned(group % chunks * tokens, tokens), tokens)]


def for_each(count, body):
    if count <= 4:
        for index in range(count):
            body(index)
        return

    def step(index, carry):
        body(index)
        return carry

    lax.fori_loop(0, count, step, 0)


def project_kernel(sizes, place_ref, block_ref, factors_ref, *refs):
    members, tokens, held, rank, experts_all = sizes
    out_ref = refs[-1]
    cores, padded = out_ref.shape[2:4]
    wide = held * rank
    chips = out_ref.shape[1]
    count = chips * held
    first = block_ref.shape[0] - members * tokens
    index = lax.broadcasted_iota(jnp.int32, (count, experts_all), 0)
    owner = place_ref[0] ^ (chips - 1 - index // held)
    owner = (owner * CORES + place_ref[1]) * held + index % held
    pick = (lax.broadcasted_iota(jnp.int32, owner.shape, 1) == owner).astype(jnp.bfloat16)
    row = lax.broadcasted_iota(jnp.int32, (padded, tokens), 0).astype(jnp.float32)
    lane = lax.broadcasted_iota(jnp.int32, (padded, wide), 1)
    if cores > 1:
        out_ref[:, :, 0] = refs[0][:, :, 0]
    batch = min(4, members)

    def one_batch(number):
        base = number * batch
        dense = [gates_of(block_ref, base + g, sizes) for g in range(batch)]
        gates = jnp.dot(pick, jnp.concatenate(dense, 1), preferred_element_type=jnp.float32)
        slot = slots_of(
            jnp.concatenate([gates[:, g * tokens : (g + 1) * tokens] for g in range(batch)])
        )
        start = aligned(first + base * tokens, 16)
        y = lax.dot_general(
            factors_ref[...],
            block_ref[pl.ds(start, batch * tokens), :],
            NT,
            preferred_element_type=jnp.float32,
        )
        weighted = [
            (y[i * rank : (i + 1) * rank] * gates[i : i + 1]).astype(jnp.bfloat16)
            for i in range(count)
        ]
        for g in range(batch):
            here = slice(g * tokens, (g + 1) * tokens)
            for k in range(chips):
                mine = range(k * held, (k + 1) * held)
                choice = [
                    jnp.where(slot[g * count + i : g * count + i + 1] == row, 1.0, 0.0)
                    for i in mine
                ]
                full = lax.dot_general(
                    jnp.concatenate(choice).astype(jnp.bfloat16),
                    jnp.concatenate([weighted[i][:, here] for i in mine]),
                    NT,
                    preferred_element_type=jnp.float32,
                )
                packed = full[:padded]
                for h in range(1, held):
                    packed = jnp.where(
                        lane >= h * rank, full[h * padded : (h + 1) * padded], packed
                    )
                out_ref[base + g, k, cores - 1] = packed.astype(jnp.bfloat16)

    for_each(members // batch, one_batch)


def project(place, block, factors, sizes, padded, before=None):
    members, tokens, held, rank, _ = sizes
    wide = held * rank
    chips = factors.shape[0] // wide
    cores = 1 if before is None else CORES
    operands = [block, factors] + ([] if before is None else [before])
    return pl.pallas_call(
        functools.partial(project_kernel, sizes),
        out_shape=jax.ShapeDtypeStruct((members, chips, cores, padded, wide), jnp.bfloat16),
        in_specs=[pl.BlockSpec(memory_space=pltpu.SMEM)]
        + [pl.BlockSpec(memory_space=pltpu.VMEM)] * len(operands),
        out_specs=pl.BlockSpec(memory_space=pltpu.VMEM),
        compiler_params=pltpu.CompilerParams(vmem_limit_bytes=VMEM),
    )(place, *operands)


def left_kernel(place_ref, *refs):
    arrived, hidden_ref, outs, rows_ref = refs[:-4], refs[-4], refs[-3:-1], refs[-1]
    for k, ref in enumerate(arrived):
        base = (place_ref[0] ^ k) * CORES
        rows_ref[base + place_ref[1]] = ref[0]
        rows_ref[base + 1 - place_ref[1]] = ref[1]
    places, capacity, wide = rows_ref.shape
    held = hidden_ref.shape[0]
    rank = wide // held
    rows = rows_ref[...].reshape(places * capacity, wide)
    half = outs[0].shape[1]
    for h in range(held):
        for index, out_ref in enumerate(outs):
            product = lax.dot_general(
                rows,
                hidden_ref[h, :, index * half : (index + 1) * half],
                TN,
                preferred_element_type=jnp.float32,
            )
            out_ref[h * rank : (h + 1) * rank] = product[h * rank : (h + 1) * rank]


def left_partial(place, arrived, own_hidden, capacity):
    held, slots, width = own_hidden.shape
    _, padded, wide = arrived[0].shape
    if padded != capacity:
        chips = len(arrived)
        rows = jnp.take(jnp.stack(arrived), jnp.arange(chips) ^ place[0], axis=0)
        rows = jnp.take(rows, jnp.arange(CORES) ^ place[1], axis=1)[:, :, :capacity]
        rows = rows.reshape(slots, held, wide // held)
        value = jnp.einsum("shr,hsf->hrf", rows, own_hidden, preferred_element_type=jnp.float32)
        value = value.reshape(wide, width)
        return [value[:, : width // 2], value[:, width // 2 :]]
    shape = jax.ShapeDtypeStruct((wide, width // 2), jnp.float32)
    return pl.pallas_call(
        left_kernel,
        out_shape=(shape, shape),
        in_specs=[pl.BlockSpec(memory_space=pltpu.SMEM)]
        + [pl.BlockSpec(memory_space=pltpu.VMEM)] * (len(arrived) + 1),
        out_specs=(pl.BlockSpec(memory_space=pltpu.VMEM),) * 2,
        scratch_shapes=[pltpu.VMEM((slots // capacity, capacity, wide), jnp.bfloat16)],
        compiler_params=pltpu.CompilerParams(vmem_limit_bytes=VMEM),
    )(place, *arrived, own_hidden)


def whiten_kernel(first_ref, first_got_ref, last_ref, last_got_ref, hidden_ref, mapped_ref, merged_ref):
    held, rank, width = merged_ref.shape
    half = width // 2
    for h in range(held):
        rows = slice(h * rank, (h + 1) * rank)
        merged_ref[h, :, :half] = first_ref[rows] + first_got_ref[rows].astype(
            jnp.float32
        )
        merged_ref[h, :, half:] = last_ref[rows] + last_got_ref[rows].astype(
            jnp.float32
        )
    lane = lax.broadcasted_iota(jnp.int32, (8, 2 * rank), 1)
    row = lax.broadcasted_iota(jnp.int32, (8, 2 * rank), 0)
    blocks = rank // 8
    states = []
    for h in range(held):
        factor = merged_ref[h]
        gram = lax.dot_general(
            factor, factor, NT, precision=HIGHEST, preferred_element_type=jnp.float32
        )
        padded = jnp.concatenate([gram, jnp.zeros_like(gram)], axis=1)
        states.append(
            [
                jnp.where(lane == rank + 8 * b + row, 1.0, padded[8 * b : 8 * b + 8])
                for b in range(blocks)
            ]
        )
    for k in range(rank):
        first, inner = k // 8, k % 8
        for state in states:
            pivot_column = jnp.broadcast_to(state[first][:, k : k + 1], (8, 2 * rank))
            scaled = state[first][inner : inner + 1] / pivot_column[inner : inner + 1]
            for b in range(first, blocks):
                column = pivot_column
                if b == first:
                    column = jnp.where(row > inner, column, 0.0)
                else:
                    column = jnp.broadcast_to(state[b][:, k : k + 1], (8, 2 * rank))
                state[b] = state[b] - column * scaled
    for h in range(held):
        inverse = []
        for b, block in enumerate(states[h]):
            pivot = jnp.sum(jnp.where(lane == 8 * b + row, block, 0.0), axis=1, keepdims=True)
            inverse.append(block[:, rank:] / jnp.sqrt(pivot))
        inverse = jnp.concatenate(inverse, axis=0)
        basis = jnp.dot(
            inverse, merged_ref[h], precision=HIGHEST, preferred_element_type=jnp.float32
        ).astype(jnp.bfloat16)
        mapped_ref[:, h * rank : (h + 1) * rank] = lax.dot_general(
            hidden_ref[h], basis, NT, preferred_element_type=jnp.float32
        ).astype(jnp.bfloat16)


def whiten_and_map(parts, own_hidden):
    held, slots, width = own_hidden.shape
    wide = parts[0].shape[0]
    return pl.pallas_call(
        whiten_kernel,
        out_shape=(
            jax.ShapeDtypeStruct((slots, wide), jnp.bfloat16),
            jax.ShapeDtypeStruct((held, wide // held, width), jnp.float32),
        ),
        compiler_params=pltpu.CompilerParams(vmem_limit_bytes=VMEM),
    )(*parts, own_hidden)


def dispatch_kernel(sizes, place_ref, block_ref, out_ref):
    members, tokens, held, _, experts_all = sizes
    count, _, padded, _ = out_ref.shape
    first = block_ref.shape[0] - members * tokens
    row = lax.broadcasted_iota(jnp.int32, (padded, tokens), 0).astype(jnp.float32)
    index = lax.broadcasted_iota(jnp.int32, (max(8, count), experts_all), 0)
    owner = place_ref[0] ^ (index // held * (2 * CORES))
    pick = lax.broadcasted_iota(jnp.int32, index.shape, 1) == owner * held + index % held
    pick = pick.astype(jnp.bfloat16)

    def one_group(g):
        gates = jnp.dot(pick, gates_of(block_ref, g, sizes), preferred_element_type=jnp.float32)
        slot = slots_of(gates)
        choice = [jnp.where(slot[i : i + 1] == row, gates[i : i + 1], 0.0) for i in range(count)]
        rows = jnp.dot(
            jnp.concatenate(choice).astype(jnp.bfloat16),
            columns_of(block_ref, first, g, sizes),
            preferred_element_type=jnp.float32,
        ).astype(jnp.bfloat16)
        for i in range(count):
            out_ref[i, g] = rows[i * padded : (i + 1) * padded]

    for_each(members, one_group)


def dispatch(place, block, sizes, padded, owners):
    members, _, held, _, _ = sizes
    return pl.pallas_call(
        functools.partial(dispatch_kernel, sizes),
        out_shape=jax.ShapeDtypeStruct(
            (owners * held, members, padded, block.shape[1]), jnp.bfloat16
        ),
        in_specs=[
            pl.BlockSpec(memory_space=pltpu.SMEM),
            pl.BlockSpec(memory_space=pltpu.VMEM),
        ],
        out_specs=pl.BlockSpec(memory_space=pltpu.VMEM),
        compiler_params=pltpu.CompilerParams(vmem_limit_bytes=VMEM),
    )(place, block)


def right_kernel(members, owner, where_ref, *refs):
    mapped, slabs, out_ref = refs[:members], refs[members:-1], refs[-1]
    held, rank, _ = out_ref.shape
    batch = min(4, members)
    for h in range(held):
        total = None
        for base in range(0, members, batch):
            groups = range(base, base + batch)
            rows = [mapped[g][where_ref[b]] for g in groups for b in range(len(slabs))]
            columns = [slab[owner * held + h, g] for g in groups for slab in slabs]
            product = lax.dot_general(
                jnp.concatenate(rows),
                jnp.concatenate(columns),
                TN,
                preferred_element_type=jnp.float32,
            )[h * rank : (h + 1) * rank]
            total = product if total is None else total + product
        out_ref[h] = total.astype(out_ref.dtype)


def right_factor(where, mapped_groups, slabs, owner, sizes, kind):
    _, _, held, rank, _ = sizes
    operands = [*mapped_groups, *slabs]
    return pl.pallas_call(
        functools.partial(right_kernel, len(mapped_groups), owner),
        out_shape=jax.ShapeDtypeStruct((held, rank, slabs[0].shape[-1]), kind),
        in_specs=[pl.BlockSpec(memory_space=pltpu.SMEM)]
        + [pl.BlockSpec(memory_space=pltpu.VMEM)] * len(operands),
        out_specs=pl.BlockSpec(memory_space=pltpu.VMEM),
        compiler_params=pltpu.CompilerParams(vmem_limit_bytes=VMEM),
    )(where, *operands)


def local(cotangent, expert_ids, gates, hidden, q_prev):
    members = lax.axis_size("dp")
    places = lax.axis_size("expert")
    chips = places // CORES
    held, _, slots, width = hidden.shape
    rank = q_prev.shape[2]
    tokens, model_width = cotangent.shape
    experts_all = held * places
    capacity = slots // places
    padded = -(-capacity // 16) * 16
    part = model_width // members
    chunks = part // tokens
    sizes = (members, tokens, held, rank, experts_all)
    my_dp = lax.axis_index("dp")
    my_place = lax.axis_index("expert")
    my_chip, my_core = my_place // CORES, my_place % CORES
    place = jnp.stack([my_chip, my_core]).astype(jnp.int32)
    own_hidden = hidden[:, 0]
    tie = lax.optimization_barrier

    def swap(block):
        return exchange(block, "expert", 1)

    pieces = cut_pieces(
        my_dp.reshape(1).astype(jnp.int32), cotangent, expert_ids, gates, members, experts_all
    )
    pieces = [exchange(piece, "dp", k) if k else piece for k, piece in enumerate(pieces)]
    factor = jnp.swapaxes(q_prev, 1, 2).reshape(held * rank, part)
    factors = [factor] + [exchange(factor, "expert", CORES * k) for k in range(1, chips)]

    factors = jnp.concatenate(factors[::-1])
    pieces, factors = tie((pieces, factors))
    tails = [piece[tokens:, :tokens] for piece in pieces]
    while len(tails) % chunks:
        tails.append(jnp.zeros_like(tails[0]))
    tails = [jnp.concatenate(tails[i : i + chunks], 1) for i in range(0, len(tails), chunks)]
    own = jnp.concatenate(tails + [piece[:tokens] for piece in pieces], axis=0)

    span = min(2, chips)
    owners = chips // span

    def spread(block):
        return dispatch(my_place.reshape(1).astype(jnp.int32), block, sizes, padded, owners)

    y = project(place, own, factors, sizes, padded)
    y, own = tie((y, own))
    other = swap(own)
    y = project(place, other, factors, sizes, padded, y)
    got = [exchange(y[d], "dp", d) for d in range(1, members)]
    slabs = [spread(own), spread(other)]
    got, slabs = tie((got, slabs))
    summed = y[0].astype(jnp.float32)
    for value in got:
        summed = summed + value.astype(jnp.float32)
    summed = summed.astype(jnp.bfloat16)[::-1]
    arrived = [summed[0]] + [exchange(summed[k], "expert", CORES * k) for k in range(1, chips)]
    parts = left_partial(place, arrived, own_hidden, capacity)
    if span > 1:
        parts, own = tie((parts, own))
        near = exchange(own, "expert", CORES)
    turns = sum_steps(members)
    rounds = len(turns[0])
    for index in range(rounds):
        if index:
            parts = [p + q.astype(jnp.float32) for p, q in zip(parts, got)]
        got = [
            exchange(p.astype(jnp.bfloat16), "dp", turn[index]) for p, turn in zip(parts, turns)
        ]
    mapped, merged = whiten_and_map([parts[0], got[0], parts[1], got[1]], own_hidden)
    mapped = mapped.reshape(places, capacity, held * rank)
    mapped = jnp.pad(mapped, ((0, 0), (0, padded - capacity), (0, 0)))
    if span > 1:
        mapped, near = tie((mapped, near))
        near_other = swap(near)

    def rows_for(chip):
        return lax.dynamic_slice_in_dim(mapped, chip // span * span * CORES, span * CORES, 0)

    def over_groups(value):
        return [value] + [exchange(value, "dp", d) for d in range(1, members)]

    sent = [
        exchange(rows_for(my_chip ^ (span * m)), "expert", span * m * CORES)
        for m in range(1, owners)
    ]
    if span > 1:
        slab = spread(near)
        if owners > 1:
            sent, slab = tie((sent, slab))
        slabs.append(slab)
    gathered = [over_groups(value) for value in sent]
    if span > 1:
        slab = spread(near_other)
        if owners > 1:
            gathered, slab = tie((gathered, slab))
        slabs.append(slab)
    where = jnp.stack([my_chip % span, my_chip % span, (my_chip ^ 1) % span, (my_chip ^ 1) % span])
    where = where * CORES + jnp.stack([my_core, 1 - my_core, my_core, 1 - my_core])
    where = where.astype(jnp.int32)

    def product(groups, owner, kind):
        return right_factor(where, groups, slabs, owner, sizes, kind)

    parts = [product(groups, m, jnp.bfloat16) for m, groups in enumerate(gathered, 1)]
    mine = rows_for(my_chip)
    if owners > 1:
        mine, parts = tie((mine, parts))
    parts = [exchange(value, "expert", span * m * CORES) for m, value in enumerate(parts, 1)]
    q_next = product(over_groups(mine), 0, jnp.float32)
    for value in parts:
        q_next = q_next + value.astype(jnp.float32)
    share = width // members
    p_share = lax.dynamic_slice_in_dim(merged, my_dp * share, share, 2)
    return (jnp.swapaxes(p_share, 1, 2), jnp.swapaxes(q_next, 1, 2))


def solution(mesh):
    placed = (
        P(("dp", "expert"), None),
        P(("dp", "expert"), None),
        P(("dp", "expert"), None),
        P("expert", "dp", None, None),
        P("expert", "dp", None),
    )
    return jax.shard_map(
        local,
        mesh=mesh,
        in_specs=placed,
        out_specs=(P("expert", "dp", None), P("expert", "dp", None)),
        check_vma=False,
    )
```

```python
import functools

import jax
import jax.numpy as jnp
from jax import lax
from jax.experimental import pallas as pl
from jax.experimental.pallas import tpu as pltpu
from jax.sharding import PartitionSpec as P

CORES = 2
PIVOTS = 4
VMEM = 16 << 20
HIGHEST = lax.Precision.HIGHEST
NT = (((1,), (1,)), ((), ()))
TN = (((0,), (0,)), ((), ()))


def exchange(value, axis, distance):
    size = lax.axis_size(axis)
    return lax.ppermute(value, axis, [(i, i ^ distance) for i in range(size)])


def pieces_kernel(place_ref, cotangent_ref, ids_ref, gates_ref, *out_refs):
    tokens = cotangent_ref.shape[0]
    part = out_refs[0].shape[1]
    experts_all = out_refs[0].shape[0] - tokens
    label = lax.broadcasted_iota(jnp.int32, (experts_all, tokens), 0)
    dense = jnp.zeros((experts_all, tokens), jnp.float32)
    for k in range(ids_ref.shape[0]):
        gate = gates_ref[k : k + 1].astype(jnp.float32)
        dense = dense + jnp.where(label == ids_ref[k : k + 1], gate, 0.0)
    dense = dense.astype(jnp.bfloat16)
    for k, out_ref in enumerate(out_refs):
        start = pl.multiple_of((place_ref[0] ^ k) * part, part)
        out_ref[:tokens] = cotangent_ref[:, pl.ds(start, part)]
        out_ref[tokens:] = jnp.zeros((experts_all, part), jnp.bfloat16)
        out_ref[tokens:, :tokens] = dense


def cut_pieces(place, cotangent, expert_ids, gates, members, experts_all):
    tokens, model_width = cotangent.shape
    shape = jax.ShapeDtypeStruct(
        (tokens + experts_all, model_width // members), jnp.bfloat16
    )
    return pl.pallas_call(
        pieces_kernel,
        out_shape=(shape,) * members,
        in_specs=[pl.BlockSpec(memory_space=pltpu.SMEM)]
        + [pl.BlockSpec(memory_space=pltpu.VMEM)] * 3,
        out_specs=(pl.BlockSpec(memory_space=pltpu.VMEM),) * members,
        compiler_params=pltpu.CompilerParams(vmem_limit_bytes=VMEM),
    )(place, cotangent, jnp.swapaxes(expert_ids, 0, 1), jnp.swapaxes(gates, 0, 1))


def stack_kernel(sizes, *refs):
    members, tokens, _, _, experts_all = sizes
    pieces, out_ref, sems = refs[:members], refs[-2], refs[-1]
    part = out_ref.shape[1]
    chunks = part // tokens
    first = out_ref.shape[0] - members * tokens
    copies = []
    for k, piece in enumerate(pieces):
        row, lane = k // chunks * experts_all, k % chunks * tokens
        copies += [
            pltpu.make_async_copy(
                piece.at[pl.ds(0, tokens)],
                out_ref.at[pl.ds(first + k * tokens, tokens)],
                sems.at[2 * k],
            ),
            pltpu.make_async_copy(
                piece.at[pl.ds(tokens, experts_all), pl.ds(0, tokens)],
                out_ref.at[pl.ds(row, experts_all), pl.ds(lane, tokens)],
                sems.at[2 * k + 1],
            ),
        ]
    for copy in copies:
        copy.start()
    used = members % chunks * tokens
    if used:
        out_ref[first - experts_all : first, used:] = jnp.zeros(
            (experts_all, part - used), out_ref.dtype
        )
    for copy in copies:
        copy.wait()


def stack_pieces(pieces, sizes):
    members, tokens, _, _, experts_all = sizes
    part = pieces[0].shape[1]
    rows = -(-members // (part // tokens)) * experts_all + members * tokens
    return pl.pallas_call(
        functools.partial(stack_kernel, sizes),
        out_shape=jax.ShapeDtypeStruct((rows, part), pieces[0].dtype),
        in_specs=[pl.BlockSpec(memory_space=pl.ANY)] * members,
        out_specs=pl.BlockSpec(memory_space=pltpu.VMEM),
        scratch_shapes=[pltpu.SemaphoreType.DMA((2 * members,))],
        compiler_params=pltpu.CompilerParams(vmem_limit_bytes=VMEM),
    )(*pieces)


def sum_steps(members):
    distances = []
    step = 1
    while step < members:
        distances.append(step)
        step *= 2
    return distances, distances[::-1]


def slots_of(gates):
    tokens = gates.shape[1]
    before = (
        lax.broadcasted_iota(jnp.int32, (tokens, tokens), 0)
        < lax.broadcasted_iota(jnp.int32, (tokens, tokens), 1)
    ).astype(jnp.bfloat16)
    named = (gates > 0).astype(jnp.bfloat16)
    slot = jnp.dot(named, before, preferred_element_type=jnp.float32)
    return jnp.where(gates > 0, slot, -1.0)


def aligned(value, multiple):
    return value if isinstance(value, int) else pl.multiple_of(value, multiple)


def columns_of(ref, first, group, sizes):
    tokens = sizes[1]
    return ref[pl.ds(aligned(first + group * tokens, 16), tokens), :]


def gates_of(ref, group, sizes):
    _, tokens, _, _, experts_all = sizes
    chunks = ref.shape[1] // tokens
    row = aligned(group // chunks * experts_all, 16)
    return ref[pl.ds(row, experts_all), pl.ds(aligned(group % chunks * tokens, tokens), tokens)]


def for_each(count, body):
    if count <= 4:
        for index in range(count):
            body(index)
        return

    def step(index, carry):
        body(index)
        return carry

    lax.fori_loop(0, count, step, 0)


def project_kernel(sizes, place_ref, block_ref, factors_ref, *refs):
    members, tokens, held, rank, experts_all = sizes
    out_ref = refs[-1]
    cores, padded = out_ref.shape[2:4]
    wide = held * rank
    chips = out_ref.shape[1]
    count = chips * held
    first = block_ref.shape[0] - members * tokens
    index = lax.broadcasted_iota(jnp.int32, (count, experts_all), 0)
    owner = place_ref[0] ^ (chips - 1 - index // held)
    owner = (owner * CORES + place_ref[1]) * held + index % held
    pick = (lax.broadcasted_iota(jnp.int32, owner.shape, 1) == owner).astype(jnp.bfloat16)
    row = lax.broadcasted_iota(jnp.int32, (padded, tokens), 0).astype(jnp.float32)
    lane = lax.broadcasted_iota(jnp.int32, (padded, wide), 1)
    if cores > 1:
        out_ref[:, :, 0] = refs[0][:, :, 0]
    batch = min(4, members)

    def one_batch(number):
        base = number * batch
        dense = [gates_of(block_ref, base + g, sizes) for g in range(batch)]
        gates = jnp.dot(pick, jnp.concatenate(dense, 1), preferred_element_type=jnp.float32)
        slot = slots_of(
            jnp.concatenate([gates[:, g * tokens : (g + 1) * tokens] for g in range(batch)])
        )
        start = aligned(first + base * tokens, 16)
        y = lax.dot_general(
            factors_ref[...],
            block_ref[pl.ds(start, batch * tokens), :],
            NT,
            preferred_element_type=jnp.float32,
        )
        weighted = [
            (y[i * rank : (i + 1) * rank] * gates[i : i + 1]).astype(jnp.bfloat16)
            for i in range(count)
        ]
        for g in range(batch):
            here = slice(g * tokens, (g + 1) * tokens)
            for k in range(chips):
                mine = range(k * held, (k + 1) * held)
                choice = [
                    jnp.where(slot[g * count + i : g * count + i + 1] == row, 1.0, 0.0)
                    for i in mine
                ]
                full = lax.dot_general(
                    jnp.concatenate(choice).astype(jnp.bfloat16),
                    jnp.concatenate([weighted[i][:, here] for i in mine]),
                    NT,
                    preferred_element_type=jnp.float32,
                )
                packed = full[:padded]
                for h in range(1, held):
                    packed = jnp.where(
                        lane >= h * rank, full[h * padded : (h + 1) * padded], packed
                    )
                out_ref[base + g, k, cores - 1] = packed.astype(jnp.bfloat16)

    for_each(members // batch, one_batch)


def project(place, block, factors, sizes, padded, before=None):
    members, tokens, held, rank, _ = sizes
    wide = held * rank
    chips = factors.shape[0] // wide
    cores = 1 if before is None else CORES
    operands = [block, factors] + ([] if before is None else [before])
    return pl.pallas_call(
        functools.partial(project_kernel, sizes),
        out_shape=jax.ShapeDtypeStruct((members, chips, cores, padded, wide), jnp.bfloat16),
        in_specs=[pl.BlockSpec(memory_space=pltpu.SMEM)]
        + [pl.BlockSpec(memory_space=pltpu.VMEM)] * len(operands),
        out_specs=pl.BlockSpec(memory_space=pltpu.VMEM),
        compiler_params=pltpu.CompilerParams(vmem_limit_bytes=VMEM),
    )(place, *operands)


def left_kernel(place_ref, *refs):
    arrived, hidden_ref, outs, rows_ref = refs[:-4], refs[-4], refs[-3:-1], refs[-1]
    for k, ref in enumerate(arrived):
        base = (place_ref[0] ^ k) * CORES
        rows_ref[base + place_ref[1]] = ref[0]
        rows_ref[base + 1 - place_ref[1]] = ref[1]
    places, capacity, wide = rows_ref.shape
    held = hidden_ref.shape[0]
    rank = wide // held
    rows = rows_ref[...].reshape(places * capacity, wide)
    half = outs[0].shape[1]
    for h in range(held):
        for index, out_ref in enumerate(outs):
            product = lax.dot_general(
                rows,
                hidden_ref[h, :, index * half : (index + 1) * half],
                TN,
                preferred_element_type=jnp.float32,
            )
            out_ref[h * rank : (h + 1) * rank] = product[h * rank : (h + 1) * rank]


def left_partial(place, arrived, own_hidden, capacity):
    held, slots, width = own_hidden.shape
    _, padded, wide = arrived[0].shape
    if padded != capacity:
        chips = len(arrived)
        rows = jnp.take(jnp.stack(arrived), jnp.arange(chips) ^ place[0], axis=0)
        rows = jnp.take(rows, jnp.arange(CORES) ^ place[1], axis=1)[:, :, :capacity]
        rows = rows.reshape(slots, held, wide // held)
        value = jnp.einsum("shr,hsf->hrf", rows, own_hidden, preferred_element_type=jnp.float32)
        value = value.reshape(wide, width)
        return [value[:, : width // 2], value[:, width // 2 :]]
    shape = jax.ShapeDtypeStruct((wide, width // 2), jnp.float32)
    return pl.pallas_call(
        left_kernel,
        out_shape=(shape, shape),
        in_specs=[pl.BlockSpec(memory_space=pltpu.SMEM)]
        + [pl.BlockSpec(memory_space=pltpu.VMEM)] * (len(arrived) + 1),
        out_specs=(pl.BlockSpec(memory_space=pltpu.VMEM),) * 2,
        scratch_shapes=[pltpu.VMEM((slots // capacity, capacity, wide), jnp.bfloat16)],
        compiler_params=pltpu.CompilerParams(vmem_limit_bytes=VMEM),
    )(place, *arrived, own_hidden)


def eliminate(state, k, first, inner, row):
    top = state[first]

    def columns_at(block):
        return [jnp.broadcast_to(block[:, k + j : k + j + 1], block.shape) for j in range(PIVOTS)]

    columns = columns_at(top)
    grid = [[column[inner + i : inner + i + 1] for column in columns] for i in range(PIVOTS)]
    lines = [top[inner + i : inner + i + 1] for i in range(PIVOTS)]
    scaled, ratio = [], []
    for p in range(PIVOTS):
        scaled.append(lines[p] / grid[p][p])
        ratio.append([value / grid[p][p] for value in grid[p]])
        for i in range(p + 1, PIVOTS):
            lines[i] = lines[i] - grid[i][p] * scaled[p]
            for j in range(p + 1, PIVOTS):
                grid[i][j] = grid[i][j] - grid[i][p] * ratio[p][j]
    for b in range(first, len(state)):
        factors = []
        for j, factor in enumerate(columns if b == first else columns_at(state[b])):
            for p in range(j):
                factor = factor - ratio[p][j] * factors[p]
            factors.append(factor)
        for j in range(PIVOTS):
            factor = factors[j]
            if b == first:
                factor = jnp.where(row > inner + j, factor, 0.0)
            state[b] = state[b] - factor * scaled[j]


def whiten_kernel(
    place_ref,
    first_ref,
    first_got_ref,
    last_ref,
    last_got_ref,
    hidden_ref,
    mapped_ref,
    share_ref,
    merged_ref,
):
    held, rank, width = merged_ref.shape
    half = width // 2
    for h in range(held):
        rows = slice(h * rank, (h + 1) * rank)
        merged_ref[h, :, :half] = first_ref[rows] + first_got_ref[rows].astype(
            jnp.float32
        )
        merged_ref[h, :, half:] = last_ref[rows] + last_got_ref[rows].astype(
            jnp.float32
        )
    kept = share_ref.shape[2]
    if kept == width:
        share_ref[...] = merged_ref[...]
    else:
        start = pl.multiple_of(place_ref[0] * kept, 128)
        share_ref[...] = merged_ref[:, :, pl.ds(start, kept)]
    lane = lax.broadcasted_iota(jnp.int32, (8, 2 * rank), 1)
    row = lax.broadcasted_iota(jnp.int32, (8, 2 * rank), 0)
    blocks = rank // 8
    states = []
    for h in range(held):
        factor = merged_ref[h]
        gram = lax.dot_general(
            factor, factor, NT, precision=HIGHEST, preferred_element_type=jnp.float32
        )
        padded = jnp.concatenate([gram, jnp.zeros_like(gram)], axis=1)
        states.append(
            [
                jnp.where(lane == rank + 8 * b + row, 1.0, padded[8 * b : 8 * b + 8])
                for b in range(blocks)
            ]
        )
    for k in range(0, rank, PIVOTS):
        first, inner = k // 8, k % 8
        for state in states:
            eliminate(state, k, first, inner, row)
    for h in range(held):
        inverse = []
        for b, block in enumerate(states[h]):
            pivot = jnp.sum(jnp.where(lane == 8 * b + row, block, 0.0), axis=1, keepdims=True)
            inverse.append(block[:, rank:] / jnp.sqrt(pivot))
        inverse = jnp.concatenate(inverse, axis=0)
        basis = jnp.dot(
            inverse, merged_ref[h], precision=HIGHEST, preferred_element_type=jnp.float32
        ).astype(jnp.bfloat16)
        mapped_ref[:, h * rank : (h + 1) * rank] = lax.dot_general(
            hidden_ref[h], basis, NT, preferred_element_type=jnp.float32
        ).astype(jnp.bfloat16)


def whiten_and_map(place, parts, own_hidden, members):
    held, slots, width = own_hidden.shape
    wide = parts[0].shape[0]
    share = width // members
    kept = share if share % 128 == 0 else width
    mapped, merged = pl.pallas_call(
        whiten_kernel,
        out_shape=(
            jax.ShapeDtypeStruct((slots, wide), jnp.bfloat16),
            jax.ShapeDtypeStruct((held, wide // held, kept), jnp.float32),
        ),
        in_specs=[pl.BlockSpec(memory_space=pltpu.SMEM)]
        + [pl.BlockSpec(memory_space=pltpu.VMEM)] * 5,
        out_specs=(pl.BlockSpec(memory_space=pltpu.VMEM),) * 2,
        scratch_shapes=[pltpu.VMEM((held, wide // held, width), jnp.float32)],
        compiler_params=pltpu.CompilerParams(vmem_limit_bytes=VMEM),
    )(place, *parts, own_hidden)
    if kept != share:
        merged = lax.dynamic_slice_in_dim(merged, place[0] * share, share, 2)
    return mapped, merged


def dispatch_kernel(sizes, place_ref, block_ref, out_ref):
    members, tokens, held, _, experts_all = sizes
    count, _, padded, _ = out_ref.shape
    first = block_ref.shape[0] - members * tokens
    row = lax.broadcasted_iota(jnp.int32, (padded, tokens), 0).astype(jnp.float32)
    index = lax.broadcasted_iota(jnp.int32, (max(8, count), experts_all), 0)
    owner = place_ref[0] ^ (index // held * (2 * CORES))
    pick = lax.broadcasted_iota(jnp.int32, index.shape, 1) == owner * held + index % held
    pick = pick.astype(jnp.bfloat16)

    def one_group(g):
        gates = jnp.dot(pick, gates_of(block_ref, g, sizes), preferred_element_type=jnp.float32)
        slot = slots_of(gates)
        choice = [jnp.where(slot[i : i + 1] == row, gates[i : i + 1], 0.0) for i in range(count)]
        rows = jnp.dot(
            jnp.concatenate(choice).astype(jnp.bfloat16),
            columns_of(block_ref, first, g, sizes),
            preferred_element_type=jnp.float32,
        ).astype(jnp.bfloat16)
        for i in range(count):
            out_ref[i, g] = rows[i * padded : (i + 1) * padded]

    for_each(members, one_group)


def dispatch(place, block, sizes, padded, owners):
    members, _, held, _, _ = sizes
    return pl.pallas_call(
        functools.partial(dispatch_kernel, sizes),
        out_shape=jax.ShapeDtypeStruct(
            (owners * held, members, padded, block.shape[1]), jnp.bfloat16
        ),
        in_specs=[
            pl.BlockSpec(memory_space=pltpu.SMEM),
            pl.BlockSpec(memory_space=pltpu.VMEM),
        ],
        out_specs=pl.BlockSpec(memory_space=pltpu.VMEM),
        compiler_params=pltpu.CompilerParams(vmem_limit_bytes=VMEM),
    )(place, block)


def right_kernel(members, owner, where_ref, *refs):
    mapped, slabs, out_ref = refs[:members], refs[members:-1], refs[-1]
    held, rank, _ = out_ref.shape
    batch = min(4, members)
    for h in range(held):
        total = None
        for base in range(0, members, batch):
            groups = range(base, base + batch)
            rows = [mapped[g][where_ref[b]] for g in groups for b in range(len(slabs))]
            columns = [slab[owner * held + h, g] for g in groups for slab in slabs]
            product = lax.dot_general(
                jnp.concatenate(rows),
                jnp.concatenate(columns),
                TN,
                preferred_element_type=jnp.float32,
            )[h * rank : (h + 1) * rank]
            total = product if total is None else total + product
        out_ref[h] = total.astype(out_ref.dtype)


def right_factor(where, mapped_groups, slabs, owner, sizes, kind):
    _, _, held, rank, _ = sizes
    operands = [*mapped_groups, *slabs]
    return pl.pallas_call(
        functools.partial(right_kernel, len(mapped_groups), owner),
        out_shape=jax.ShapeDtypeStruct((held, rank, slabs[0].shape[-1]), kind),
        in_specs=[pl.BlockSpec(memory_space=pltpu.SMEM)]
        + [pl.BlockSpec(memory_space=pltpu.VMEM)] * len(operands),
        out_specs=pl.BlockSpec(memory_space=pltpu.VMEM),
        compiler_params=pltpu.CompilerParams(vmem_limit_bytes=VMEM),
    )(where, *operands)


def local(cotangent, expert_ids, gates, hidden, q_prev):
    members = lax.axis_size("dp")
    places = lax.axis_size("expert")
    chips = places // CORES
    held, _, slots, width = hidden.shape
    rank = q_prev.shape[2]
    tokens, model_width = cotangent.shape
    experts_all = held * places
    capacity = slots // places
    padded = -(-capacity // 16) * 16
    part = model_width // members
    sizes = (members, tokens, held, rank, experts_all)
    my_dp = lax.axis_index("dp")
    my_place = lax.axis_index("expert")
    my_chip, my_core = my_place // CORES, my_place % CORES
    place = jnp.stack([my_chip, my_core]).astype(jnp.int32)
    own_hidden = hidden[:, 0]
    tie = lax.optimization_barrier

    def swap(block):
        return exchange(block, "expert", 1)

    dp_place = my_dp.reshape(1).astype(jnp.int32)
    pieces = cut_pieces(dp_place, cotangent, expert_ids, gates, members, experts_all)
    pieces = [exchange(piece, "dp", k) if k else piece for k, piece in enumerate(pieces)]
    factor = jnp.swapaxes(q_prev, 1, 2).reshape(held * rank, part)
    factors = [factor] + [exchange(factor, "expert", CORES * k) for k in range(1, chips)]

    factors = jnp.concatenate(factors[::-1])
    pieces, factors = tie((pieces, factors))
    own = stack_pieces(pieces, sizes)

    span = min(2, chips)
    owners = chips // span

    def spread(block):
        return dispatch(my_place.reshape(1).astype(jnp.int32), block, sizes, padded, owners)

    y = project(place, own, factors, sizes, padded)
    y, own = tie((y, own))
    other = swap(own)
    y = project(place, other, factors, sizes, padded, y)
    got = [exchange(y[d], "dp", d) for d in range(1, members)]
    slabs = [spread(own), spread(other)]
    got, slabs = tie((got, slabs))
    summed = y[0].astype(jnp.float32)
    for value in got:
        summed = summed + value.astype(jnp.float32)
    summed = summed.astype(jnp.bfloat16)[::-1]
    arrived = [summed[0]] + [exchange(summed[k], "expert", CORES * k) for k in range(1, chips)]
    if span > 1:
        arrived, own = tie((arrived, own))
        near = exchange(own, "expert", CORES)
    parts = left_partial(place, arrived, own_hidden, capacity)
    turns = sum_steps(members)
    rounds = len(turns[0])
    for index in range(rounds):
        if index:
            parts = [p + q.astype(jnp.float32) for p, q in zip(parts, got)]
        got = [
            exchange(p.astype(jnp.bfloat16), "dp", turn[index]) for p, turn in zip(parts, turns)
        ]
    mapped, p_share = whiten_and_map(
        dp_place, [parts[0], got[0], parts[1], got[1]], own_hidden, members
    )
    mapped = mapped.reshape(places, capacity, held * rank)
    mapped = jnp.pad(mapped, ((0, 0), (0, padded - capacity), (0, 0)))
    if span > 1:
        mapped, near = tie((mapped, near))
        near_other = swap(near)

    def rows_for(chip):
        return lax.dynamic_slice_in_dim(mapped, chip // span * span * CORES, span * CORES, 0)

    def over_groups(value):
        return [value] + [exchange(value, "dp", d) for d in range(1, members)]

    sent = [
        exchange(rows_for(my_chip ^ (span * m)), "expert", span * m * CORES)
        for m in range(1, owners)
    ]
    if span > 1:
        slab = spread(near)
        if owners > 1:
            sent, slab = tie((sent, slab))
        slabs.append(slab)
    gathered = [over_groups(value) for value in sent]
    if span > 1:
        slab = spread(near_other)
        if owners > 1:
            gathered, slab = tie((gathered, slab))
        slabs.append(slab)
    where = jnp.stack([my_chip % span, my_chip % span, (my_chip ^ 1) % span, (my_chip ^ 1) % span])
    where = where * CORES + jnp.stack([my_core, 1 - my_core, my_core, 1 - my_core])
    where = where.astype(jnp.int32)

    def product(groups, owner, kind):
        return right_factor(where, groups, slabs, owner, sizes, kind)

    parts = [product(groups, m, jnp.bfloat16) for m, groups in enumerate(gathered, 1)]
    mine = rows_for(my_chip)
    if owners > 1:
        mine, parts = tie((mine, parts))
    parts = [exchange(value, "expert", span * m * CORES) for m, value in enumerate(parts, 1)]
    q_next = product(over_groups(mine), 0, jnp.float32)
    for value in parts:
        q_next = q_next + value.astype(jnp.float32)
    return (jnp.swapaxes(p_share, 1, 2), jnp.swapaxes(q_next, 1, 2))


def solution(mesh):
    placed = (
        P(("dp", "expert"), None),
        P(("dp", "expert"), None),
        P(("dp", "expert"), None),
        P("expert", "dp", None, None),
        P("expert", "dp", None),
    )
    return jax.shard_map(
        local,
        mesh=mesh,
        in_specs=placed,
        out_specs=(P("expert", "dp", None), P("expert", "dp", None)),
        check_vma=False,
    )
```

```python
import functools

import jax
import jax.numpy as jnp
from jax import lax
from jax.experimental import pallas as pl
from jax.experimental.pallas import tpu as pltpu
from jax.sharding import PartitionSpec as P

CORES = 2
PIVOTS = 4
VMEM = 32 << 20
HIGHEST = lax.Precision.HIGHEST
NT = (((1,), (1,)), ((), ()))
TN = (((0,), (0,)), ((), ()))


def exchange(value, axis, distance):
    size = lax.axis_size(axis)
    return lax.ppermute(value, axis, [(i, i ^ distance) for i in range(size)])


def pieces_kernel(place_ref, cotangent_ref, ids_ref, gates_ref, *out_refs):
    tokens = cotangent_ref.shape[0]
    part = out_refs[0].shape[1]
    experts_all = out_refs[0].shape[0] - tokens
    label = lax.broadcasted_iota(jnp.int32, (experts_all, tokens), 0)
    dense = jnp.zeros((experts_all, tokens), jnp.float32)
    for k in range(ids_ref.shape[0]):
        gate = gates_ref[k : k + 1].astype(jnp.float32)
        dense = dense + jnp.where(label == ids_ref[k : k + 1], gate, 0.0)
    dense = dense.astype(jnp.bfloat16)
    for k, out_ref in enumerate(out_refs):
        start = pl.multiple_of((place_ref[0] ^ k) * part, part)
        out_ref[:tokens] = cotangent_ref[:, pl.ds(start, part)]
        out_ref[tokens:] = jnp.zeros((experts_all, part), jnp.bfloat16)
        out_ref[tokens:, :tokens] = dense


def cut_pieces(place, cotangent, expert_ids, gates, members, experts_all):
    tokens, model_width = cotangent.shape
    shape = jax.ShapeDtypeStruct(
        (tokens + experts_all, model_width // members), jnp.bfloat16
    )
    return pl.pallas_call(
        pieces_kernel,
        out_shape=(shape,) * members,
        in_specs=[pl.BlockSpec(memory_space=pltpu.SMEM)]
        + [pl.BlockSpec(memory_space=pltpu.VMEM)] * 3,
        out_specs=(pl.BlockSpec(memory_space=pltpu.VMEM),) * members,
        compiler_params=pltpu.CompilerParams(vmem_limit_bytes=VMEM),
    )(place, cotangent, jnp.swapaxes(expert_ids, 0, 1), jnp.swapaxes(gates, 0, 1))


def stack_kernel(sizes, *refs):
    members, tokens, _, _, experts_all = sizes
    pieces, out_ref, sems = refs[:members], refs[-2], refs[-1]
    part = out_ref.shape[1]
    chunks = part // tokens
    first = out_ref.shape[0] - members * tokens
    copies = []
    for k, piece in enumerate(pieces):
        row, lane = k // chunks * experts_all, k % chunks * tokens
        copies += [
            pltpu.make_async_copy(
                piece.at[pl.ds(0, tokens)],
                out_ref.at[pl.ds(first + k * tokens, tokens)],
                sems.at[2 * k],
            ),
            pltpu.make_async_copy(
                piece.at[pl.ds(tokens, experts_all), pl.ds(0, tokens)],
                out_ref.at[pl.ds(row, experts_all), pl.ds(lane, tokens)],
                sems.at[2 * k + 1],
            ),
        ]
    for copy in copies:
        copy.start()
    used = members % chunks * tokens
    if used:
        out_ref[first - experts_all : first, used:] = jnp.zeros(
            (experts_all, part - used), out_ref.dtype
        )
    for copy in copies:
        copy.wait()


def stack_pieces(pieces, sizes):
    members, tokens, _, _, experts_all = sizes
    part = pieces[0].shape[1]
    rows = -(-members // (part // tokens)) * experts_all + members * tokens
    return pl.pallas_call(
        functools.partial(stack_kernel, sizes),
        out_shape=jax.ShapeDtypeStruct((rows, part), pieces[0].dtype),
        in_specs=[pl.BlockSpec(memory_space=pl.ANY)] * members,
        out_specs=pl.BlockSpec(memory_space=pltpu.VMEM),
        scratch_shapes=[pltpu.SemaphoreType.DMA((2 * members,))],
        compiler_params=pltpu.CompilerParams(vmem_limit_bytes=VMEM),
    )(*pieces)


def sum_steps(members):
    distances = []
    step = 1
    while step < members:
        distances.append(step)
        step *= 2
    return distances, distances[::-1]


def slots_of(gates):
    tokens = gates.shape[1]
    before = (
        lax.broadcasted_iota(jnp.int32, (tokens, tokens), 0)
        < lax.broadcasted_iota(jnp.int32, (tokens, tokens), 1)
    ).astype(jnp.bfloat16)
    named = (gates > 0).astype(jnp.bfloat16)
    slot = jnp.dot(named, before, preferred_element_type=jnp.float32)
    return jnp.where(gates > 0, slot, -1.0)


def aligned(value, multiple):
    return value if isinstance(value, int) else pl.multiple_of(value, multiple)


def columns_of(ref, first, group, sizes):
    tokens = sizes[1]
    return ref[pl.ds(aligned(first + group * tokens, 16), tokens), :]


def gates_of(ref, group, sizes):
    _, tokens, _, _, experts_all = sizes
    chunks = ref.shape[1] // tokens
    row = aligned(group // chunks * experts_all, 16)
    return ref[pl.ds(row, experts_all), pl.ds(aligned(group % chunks * tokens, tokens), tokens)]


def for_each(count, body):
    if count <= 4:
        for index in range(count):
            body(index)
        return

    def step(index, carry):
        body(index)
        return carry

    lax.fori_loop(0, count, step, 0)


def project_kernel(sizes, place_ref, block_ref, factors_ref, *refs):
    members, tokens, held, rank, experts_all = sizes
    out_ref = refs[-1]
    cores, padded = out_ref.shape[2:4]
    wide = held * rank
    chips = out_ref.shape[1]
    count = chips * held
    first = block_ref.shape[0] - members * tokens
    index = lax.broadcasted_iota(jnp.int32, (count, experts_all), 0)
    owner = place_ref[0] ^ (chips - 1 - index // held)
    owner = (owner * CORES + place_ref[1]) * held + index % held
    pick = (lax.broadcasted_iota(jnp.int32, owner.shape, 1) == owner).astype(jnp.bfloat16)
    row = lax.broadcasted_iota(jnp.int32, (padded, tokens), 0).astype(jnp.float32)
    lane = lax.broadcasted_iota(jnp.int32, (padded, wide), 1)
    if cores > 1:
        out_ref[:, :, 0] = refs[0][:, :, 0]
    batch = min(4, members)

    def one_batch(number):
        base = number * batch
        dense = [gates_of(block_ref, base + g, sizes) for g in range(batch)]
        gates = jnp.dot(pick, jnp.concatenate(dense, 1), preferred_element_type=jnp.float32)
        slot = slots_of(
            jnp.concatenate([gates[:, g * tokens : (g + 1) * tokens] for g in range(batch)])
        )
        start = aligned(first + base * tokens, 16)
        y = lax.dot_general(
            factors_ref[...],
            block_ref[pl.ds(start, batch * tokens), :],
            NT,
            preferred_element_type=jnp.float32,
        )
        weighted = [
            (y[i * rank : (i + 1) * rank] * gates[i : i + 1]).astype(jnp.bfloat16)
            for i in range(count)
        ]
        for g in range(batch):
            here = slice(g * tokens, (g + 1) * tokens)
            for k in range(chips):
                mine = range(k * held, (k + 1) * held)
                choice = [
                    jnp.where(slot[g * count + i : g * count + i + 1] == row, 1.0, 0.0)
                    for i in mine
                ]
                full = lax.dot_general(
                    jnp.concatenate(choice).astype(jnp.bfloat16),
                    jnp.concatenate([weighted[i][:, here] for i in mine]),
                    NT,
                    preferred_element_type=jnp.float32,
                )
                packed = full[:padded]
                for h in range(1, held):
                    packed = jnp.where(
                        lane >= h * rank, full[h * padded : (h + 1) * padded], packed
                    )
                out_ref[base + g, k, cores - 1] = packed.astype(jnp.bfloat16)

    for_each(members // batch, one_batch)


def project(place, block, factors, sizes, padded, before=None):
    members, tokens, held, rank, _ = sizes
    wide = held * rank
    chips = factors.shape[0] // wide
    cores = 1 if before is None else CORES
    operands = [block, factors] + ([] if before is None else [before])
    return pl.pallas_call(
        functools.partial(project_kernel, sizes),
        out_shape=jax.ShapeDtypeStruct((members, chips, cores, padded, wide), jnp.bfloat16),
        in_specs=[pl.BlockSpec(memory_space=pltpu.SMEM)]
        + [pl.BlockSpec(memory_space=pltpu.VMEM)] * len(operands),
        out_specs=pl.BlockSpec(memory_space=pltpu.VMEM),
        compiler_params=pltpu.CompilerParams(vmem_limit_bytes=VMEM),
    )(place, *operands)


def left_kernel(place_ref, *refs):
    arrived, hidden_ref, outs, rows_ref = refs[:-4], refs[-4], refs[-3:-1], refs[-1]
    for k, ref in enumerate(arrived):
        base = (place_ref[0] ^ k) * CORES
        rows_ref[base + place_ref[1]] = ref[0]
        rows_ref[base + 1 - place_ref[1]] = ref[1]
    places, capacity, wide = rows_ref.shape
    held = hidden_ref.shape[0]
    rank = wide // held
    rows = rows_ref[...].reshape(places * capacity, wide)
    half = outs[0].shape[1]
    for h in range(held):
        for index, out_ref in enumerate(outs):
            product = lax.dot_general(
                rows,
                hidden_ref[h, :, index * half : (index + 1) * half],
                TN,
                preferred_element_type=jnp.float32,
            )
            out_ref[h * rank : (h + 1) * rank] = product[h * rank : (h + 1) * rank]


def left_partial(place, arrived, own_hidden, capacity):
    held, slots, width = own_hidden.shape
    _, padded, wide = arrived[0].shape
    if padded != capacity:
        chips = len(arrived)
        rows = jnp.take(jnp.stack(arrived), jnp.arange(chips) ^ place[0], axis=0)
        rows = jnp.take(rows, jnp.arange(CORES) ^ place[1], axis=1)[:, :, :capacity]
        rows = rows.reshape(slots, held, wide // held)
        value = jnp.einsum("shr,hsf->hrf", rows, own_hidden, preferred_element_type=jnp.float32)
        value = value.reshape(wide, width)
        return [value[:, : width // 2], value[:, width // 2 :]]
    shape = jax.ShapeDtypeStruct((wide, width // 2), jnp.float32)
    return pl.pallas_call(
        left_kernel,
        out_shape=(shape, shape),
        in_specs=[pl.BlockSpec(memory_space=pltpu.SMEM)]
        + [pl.BlockSpec(memory_space=pltpu.VMEM)] * (len(arrived) + 1),
        out_specs=(pl.BlockSpec(memory_space=pltpu.VMEM),) * 2,
        scratch_shapes=[pltpu.VMEM((slots // capacity, capacity, wide), jnp.bfloat16)],
        compiler_params=pltpu.CompilerParams(vmem_limit_bytes=VMEM),
    )(place, *arrived, own_hidden)


def eliminate(state, k, first, inner, row):
    top = state[first]

    def columns_at(block):
        return [jnp.broadcast_to(block[:, k + j : k + j + 1], block.shape) for j in range(PIVOTS)]

    columns = columns_at(top)
    grid = [[column[inner + i : inner + i + 1] for column in columns] for i in range(PIVOTS)]
    lines = [top[inner + i : inner + i + 1] for i in range(PIVOTS)]
    scaled, ratio = [], []
    for p in range(PIVOTS):
        scaled.append(lines[p] / grid[p][p])
        ratio.append([value / grid[p][p] for value in grid[p]])
        for i in range(p + 1, PIVOTS):
            lines[i] = lines[i] - grid[i][p] * scaled[p]
            for j in range(p + 1, PIVOTS):
                grid[i][j] = grid[i][j] - grid[i][p] * ratio[p][j]
    for b in range(first, len(state)):
        factors = []
        for j, factor in enumerate(columns if b == first else columns_at(state[b])):
            for p in range(j):
                factor = factor - ratio[p][j] * factors[p]
            factors.append(factor)
        for j in range(PIVOTS):
            factor = factors[j]
            if b == first:
                factor = jnp.where(row > inner + j, factor, 0.0)
            state[b] = state[b] - factor * scaled[j]


def whiten_kernel(
    place_ref,
    first_ref,
    first_got_ref,
    last_ref,
    last_got_ref,
    hidden_ref,
    mapped_ref,
    share_ref,
    merged_ref,
):
    held, rank, width = merged_ref.shape
    half = width // 2
    for h in range(held):
        rows = slice(h * rank, (h + 1) * rank)
        merged_ref[h, :, :half] = first_ref[rows] + first_got_ref[rows].astype(
            jnp.float32
        )
        merged_ref[h, :, half:] = last_ref[rows] + last_got_ref[rows].astype(
            jnp.float32
        )
    kept = share_ref.shape[2]
    if kept == width:
        share_ref[...] = merged_ref[...]
    else:
        start = pl.multiple_of(place_ref[0] * kept, 128)
        share_ref[...] = merged_ref[:, :, pl.ds(start, kept)]
    lane = lax.broadcasted_iota(jnp.int32, (8, 2 * rank), 1)
    row = lax.broadcasted_iota(jnp.int32, (8, 2 * rank), 0)
    blocks = rank // 8
    states = []
    for h in range(held):
        factor = merged_ref[h]
        gram = lax.dot_general(
            factor, factor, NT, precision=HIGHEST, preferred_element_type=jnp.float32
        )
        padded = jnp.concatenate([gram, jnp.zeros_like(gram)], axis=1)
        states.append(
            [
                jnp.where(lane == rank + 8 * b + row, 1.0, padded[8 * b : 8 * b + 8])
                for b in range(blocks)
            ]
        )
    for k in range(0, rank, PIVOTS):
        first, inner = k // 8, k % 8
        for state in states:
            eliminate(state, k, first, inner, row)
    for h in range(held):
        inverse = []
        for b, block in enumerate(states[h]):
            pivot = jnp.sum(jnp.where(lane == 8 * b + row, block, 0.0), axis=1, keepdims=True)
            inverse.append(block[:, rank:] / jnp.sqrt(pivot))
        inverse = jnp.concatenate(inverse, axis=0)
        basis = jnp.dot(
            inverse, merged_ref[h], precision=HIGHEST, preferred_element_type=jnp.float32
        ).astype(jnp.bfloat16)
        mapped_ref[:, h * rank : (h + 1) * rank] = lax.dot_general(
            hidden_ref[h], basis, NT, preferred_element_type=jnp.float32
        ).astype(jnp.bfloat16)


def whiten_and_map(place, parts, own_hidden, members):
    held, slots, width = own_hidden.shape
    wide = parts[0].shape[0]
    share = width // members
    kept = share if share % 128 == 0 else width
    mapped, merged = pl.pallas_call(
        whiten_kernel,
        out_shape=(
            jax.ShapeDtypeStruct((slots, wide), jnp.bfloat16),
            jax.ShapeDtypeStruct((held, wide // held, kept), jnp.float32),
        ),
        in_specs=[pl.BlockSpec(memory_space=pltpu.SMEM)]
        + [pl.BlockSpec(memory_space=pltpu.VMEM)] * 5,
        out_specs=(pl.BlockSpec(memory_space=pltpu.VMEM),) * 2,
        scratch_shapes=[pltpu.VMEM((held, wide // held, width), jnp.float32)],
        compiler_params=pltpu.CompilerParams(vmem_limit_bytes=VMEM),
    )(place, *parts, own_hidden)
    if kept != share:
        merged = lax.dynamic_slice_in_dim(merged, place[0] * share, share, 2)
    return mapped, merged


def dispatch_kernel(sizes, place_ref, block_ref, out_ref):
    members, tokens, held, _, experts_all = sizes
    count, _, padded, _ = out_ref.shape
    first = block_ref.shape[0] - members * tokens
    row = lax.broadcasted_iota(jnp.int32, (padded, tokens), 0).astype(jnp.float32)
    index = lax.broadcasted_iota(jnp.int32, (max(8, count), experts_all), 0)
    owner = place_ref[0] ^ (index // held * (2 * CORES))
    pick = lax.broadcasted_iota(jnp.int32, index.shape, 1) == owner * held + index % held
    pick = pick.astype(jnp.bfloat16)

    def one_group(g):
        gates = jnp.dot(pick, gates_of(block_ref, g, sizes), preferred_element_type=jnp.float32)
        slot = slots_of(gates)
        choice = [jnp.where(slot[i : i + 1] == row, gates[i : i + 1], 0.0) for i in range(count)]
        rows = jnp.dot(
            jnp.concatenate(choice).astype(jnp.bfloat16),
            columns_of(block_ref, first, g, sizes),
            preferred_element_type=jnp.float32,
        ).astype(jnp.bfloat16)
        for i in range(count):
            out_ref[i, g] = rows[i * padded : (i + 1) * padded]

    for_each(members, one_group)


def dispatch(place, block, sizes, padded, owners):
    members, _, held, _, _ = sizes
    return pl.pallas_call(
        functools.partial(dispatch_kernel, sizes),
        out_shape=jax.ShapeDtypeStruct(
            (owners * held, members, padded, block.shape[1]), jnp.bfloat16
        ),
        in_specs=[
            pl.BlockSpec(memory_space=pltpu.SMEM),
            pl.BlockSpec(memory_space=pltpu.VMEM),
        ],
        out_specs=pl.BlockSpec(memory_space=pltpu.VMEM),
        compiler_params=pltpu.CompilerParams(vmem_limit_bytes=VMEM),
    )(place, block)


def right_kernel(members, owner, where_ref, *refs):
    mapped, slabs, out_ref = refs[:members], refs[members:-1], refs[-1]
    held, rank, _ = out_ref.shape
    batch = min(4, members)
    for h in range(held):
        total = None
        for base in range(0, members, batch):
            groups = range(base, base + batch)
            rows = [mapped[g][where_ref[b]] for g in groups for b in range(len(slabs))]
            columns = [slab[owner * held + h, g] for g in groups for slab in slabs]
            product = lax.dot_general(
                jnp.concatenate(rows),
                jnp.concatenate(columns),
                TN,
                preferred_element_type=jnp.float32,
            )[h * rank : (h + 1) * rank]
            total = product if total is None else total + product
        out_ref[h] = total.astype(out_ref.dtype)


def right_factor(where, mapped_groups, slabs, owner, sizes, kind):
    _, _, held, rank, _ = sizes
    operands = [*mapped_groups, *slabs]
    return pl.pallas_call(
        functools.partial(right_kernel, len(mapped_groups), owner),
        out_shape=jax.ShapeDtypeStruct((held, rank, slabs[0].shape[-1]), kind),
        in_specs=[pl.BlockSpec(memory_space=pltpu.SMEM)]
        + [pl.BlockSpec(memory_space=pltpu.VMEM)] * len(operands),
        out_specs=pl.BlockSpec(memory_space=pltpu.VMEM),
        compiler_params=pltpu.CompilerParams(vmem_limit_bytes=VMEM),
    )(where, *operands)


def local(cotangent, expert_ids, gates, hidden, q_prev):
    members = lax.axis_size("dp")
    places = lax.axis_size("expert")
    chips = places // CORES
    held, _, slots, width = hidden.shape
    rank = q_prev.shape[2]
    tokens, model_width = cotangent.shape
    experts_all = held * places
    capacity = slots // places
    padded = -(-capacity // 16) * 16
    part = model_width // members
    sizes = (members, tokens, held, rank, experts_all)
    my_dp = lax.axis_index("dp")
    my_place = lax.axis_index("expert")
    my_chip, my_core = my_place // CORES, my_place % CORES
    place = jnp.stack([my_chip, my_core]).astype(jnp.int32)
    own_hidden = hidden[:, 0]
    tie = lax.optimization_barrier

    def swap(block):
        return exchange(block, "expert", 1)

    dp_place = my_dp.reshape(1).astype(jnp.int32)
    pieces = cut_pieces(dp_place, cotangent, expert_ids, gates, members, experts_all)
    pieces = [exchange(piece, "dp", k) if k else piece for k, piece in enumerate(pieces)]
    factor = jnp.swapaxes(q_prev, 1, 2).reshape(held * rank, part)
    factors = [factor] + [exchange(factor, "expert", CORES * k) for k in range(1, chips)]

    factors = jnp.concatenate(factors[::-1])
    pieces, factors = tie((pieces, factors))
    own = stack_pieces(pieces, sizes)

    span = min(2, chips)
    owners = chips // span

    def spread(block):
        return dispatch(my_place.reshape(1).astype(jnp.int32), block, sizes, padded, owners)

    y = project(place, own, factors, sizes, padded)
    y, own = tie((y, own))
    other = swap(own)
    y = project(place, other, factors, sizes, padded, y)
    got = [exchange(y[d], "dp", d) for d in range(1, members)]
    slabs = [spread(own), spread(other)]
    got, slabs = tie((got, slabs))
    summed = y[0].astype(jnp.float32)
    for value in got:
        summed = summed + value.astype(jnp.float32)
    summed = summed.astype(jnp.bfloat16)[::-1]
    arrived = [summed[0]] + [exchange(summed[k], "expert", CORES * k) for k in range(1, chips)]
    parts = left_partial(place, arrived, own_hidden, capacity)
    if span > 1:
        _, near = tie((arrived, own))
        near = exchange(near, "expert", CORES)
    turns = sum_steps(members)
    rounds = len(turns[0])
    for index in range(rounds):
        if index:
            parts = [p + q.astype(jnp.float32) for p, q in zip(parts, got)]
        got = [
            exchange(p.astype(jnp.bfloat16), "dp", turn[index]) for p, turn in zip(parts, turns)
        ]
    mapped, p_share = whiten_and_map(
        dp_place, [parts[0], got[0], parts[1], got[1]], own_hidden, members
    )
    mapped = mapped.reshape(places, capacity, held * rank)
    mapped = jnp.pad(mapped, ((0, 0), (0, padded - capacity), (0, 0)))
    if span > 1:
        mapped, near = tie((mapped, near))
        near_other = swap(near)

    def rows_for(chip):
        return lax.dynamic_slice_in_dim(mapped, chip // span * span * CORES, span * CORES, 0)

    def over_groups(value):
        return [value] + [exchange(value, "dp", d) for d in range(1, members)]

    sent = [
        exchange(rows_for(my_chip ^ (span * m)), "expert", span * m * CORES)
        for m in range(1, owners)
    ]
    if span > 1:
        slab = spread(near)
        if owners > 1:
            sent, slab = tie((sent, slab))
        slabs.append(slab)
    gathered = [over_groups(value) for value in sent]
    if span > 1:
        slab = spread(near_other)
        if owners > 1:
            gathered, slab = tie((gathered, slab))
        slabs.append(slab)
    where = jnp.stack([my_chip % span, my_chip % span, (my_chip ^ 1) % span, (my_chip ^ 1) % span])
    where = where * CORES + jnp.stack([my_core, 1 - my_core, my_core, 1 - my_core])
    where = where.astype(jnp.int32)

    def product(groups, owner, kind):
        return right_factor(where, groups, slabs, owner, sizes, kind)

    parts = [product(groups, m, jnp.bfloat16) for m, groups in enumerate(gathered, 1)]
    mine = rows_for(my_chip)
    if owners > 1:
        mine, parts = tie((mine, parts))
    parts = [exchange(value, "expert", span * m * CORES) for m, value in enumerate(parts, 1)]
    q_next = product(over_groups(mine), 0, jnp.float32)
    for value in parts:
        q_next = q_next + value.astype(jnp.float32)
    return (jnp.swapaxes(p_share, 1, 2), jnp.swapaxes(q_next, 1, 2))


def solution(mesh):
    placed = (
        P(("dp", "expert"), None),
        P(("dp", "expert"), None),
        P(("dp", "expert"), None),
        P("expert", "dp", None, None),
        P("expert", "dp", None),
    )
    return jax.shard_map(
        local,
        mesh=mesh,
        in_specs=placed,
        out_specs=(P("expert", "dp", None), P("expert", "dp", None)),
        check_vma=False,
    )
```
